32 devices in a mesh: rep: 8 (over y, x, core), fsdp: 4 (over z).
Axes of the slice: x: 2, y: 2, z: 4, core: 2. Of those that a mesh axis runs over, the one named last changes fastest.
Arguments:
- tokens: bfloat16 [4096, 4096], P(('rep', 'fsdp')), may hold values from -6 to 6
- queries: bfloat16 [4096, 2048], P(('rep', 'fsdp')), may hold values from -10 to 10
- rotated_key_rows: bfloat16 [4096, 512], P(('rep', 'fsdp')), may hold values from -3 to 3
- targets: bfloat16 [4096, 2048], P(('rep', 'fsdp')), may hold values from -6 to 6
- value_weights: float32 [4096, 512], P('fsdp'), may hold values from -4 to 4
- momentum: float32 [4096, 512], P('fsdp'), may hold values from -0.6 to 0.6
- first_moment: float32 [8, 4096, 512], P('rep', 'fsdp'), may hold values from -1.8 to 1.8
- second_moment: float32 [8, 4096, 512], P('rep', 'fsdp'), may hold values from 0.02 to 0.5
Outputs:
- new_weights: float32 [4096, 512], P('fsdp')
- new_momentum: float32 [4096, 512], P('fsdp')
The draws below stay inside these ranges and needn't reach their ends.
All inputs are finite; a program needn't handle non-finite values.
Results may differ from the reference program's by a relative error of at most 0.0045.
Values may be sent and summed in bfloat16 or wider, within the bound.
No kernel may reach another device: no remote copies, remote signals or barrier semaphores. Data moves between devices by JAX's collectives and lax.ppermute only.
A program may use at most 64 MiB of HBM per device.

```python
import math
import jax
import jax.numpy as jnp
from jax import lax

D = 4096
LOCAL_QUERY_HEADS = 16
LOCAL_KEY_HEADS = 4
HEAD_SIZE = 128
DEVICE_TOKENS = 128
KVW = 512
QW = 2048
RTOK = 512
REPLICAS = 8
TOTAL_TOKENS = 4096
N_REP = 8
N_FSDP = 4


def attention_couple(key):
    base = jax.random.fold_in(key, 11)
    key_query, key_random_keys = jax.random.split(base, 2)
    queries = jax.random.truncated_normal(key_query, -4.0, 4.0, (TOTAL_TOKENS, LOCAL_QUERY_HEADS, HEAD_SIZE), jnp.float32)
    rotated_key_rows = jax.random.truncated_normal(key_random_keys, -3.0, 3.0, (TOTAL_TOKENS, LOCAL_KEY_HEADS, HEAD_SIZE), jnp.float32)
    return (queries, rotated_key_rows)


def draw_queries(key, part):
    return attention_couple(key)[0].reshape(TOTAL_TOKENS, LOCAL_QUERY_HEADS * HEAD_SIZE).astype(jnp.bfloat16)


def draw_rotated_key_rows(key, part):
    return attention_couple(key)[1].reshape(TOTAL_TOKENS, LOCAL_KEY_HEADS * HEAD_SIZE).astype(jnp.bfloat16)


def shard_levels(key, extent, shards, least, top_value):
    factor_of = 1.0
    for axis_at, shards_of in shards:
        draws = jax.random.uniform(jax.random.fold_in(jax.random.fold_in(key, 6), axis_at), (shards_of,), jnp.float32, least / len(shards), top_value / len(shards))
        factor_of = factor_of * jnp.repeat(jnp.exp(draws), extent[axis_at] // shards_of).reshape((-1,) + (1,) * (len(extent) - 1 - axis_at))
    return factor_of


def scatter_about(rng, extent, width, reach, shards=(), kind=jnp.bfloat16):
    level = shard_levels(rng, extent, shards, -0.22, 0.18) if shards else 1.0
    result = jax.random.normal(rng, extent, jnp.float32) * width * level
    return jnp.minimum(jnp.maximum(result, -reach), reach).astype(kind)


def setup_inputs(seed: int = 0) -> dict:
    streams_of = jax.random.split(jax.random.key(seed), 9)
    return {
        "tokens": scatter_about(streams_of[0], (TOTAL_TOKENS, D), 1.0, 6.0, ((0, 32),)),
        "queries": draw_queries(jax.random.fold_in(streams_of[8], 71), 0),
        "rotated_key_rows": draw_rotated_key_rows(jax.random.fold_in(streams_of[8], 71), 0),
        "targets": scatter_about(streams_of[3], (TOTAL_TOKENS, QW), 1.0, 6.0, ((0, 32),)),
        "value_weights": scatter_about(streams_of[4], (D, KVW), 1.0, 4.0, ((0, 4),), jnp.float32),
        "momentum": scatter_about(streams_of[5], (D, KVW), 0.1, 0.6, ((0, 4),), jnp.float32),
        "first_moment": scatter_about(streams_of[6], (REPLICAS, D, KVW), 0.3, 1.8, ((0, 8), (1, 4)), jnp.float32),
        "second_moment": jnp.clip(jnp.exp(math.log(0.5) - 3.218876 * jax.random.uniform(streams_of[7], (REPLICAS, D, KVW), jnp.float32) ** shard_levels(streams_of[7], (REPLICAS, D, KVW), ((0, 8), (1, 4)), -0.2, 0.2)), 0.02, 0.5),
    }


first_decay = 0.9
second_decay = 0.95
weight_decay = 0.1
inner_rate = 0.05
outer_rate = 0.7
momentum_keep = 0.9
epsilon = 1e-08

def reference(tokens, queries, rotated_key_rows, targets, value_weights, momentum, first_moment, second_moment):
    heads_per_group = LOCAL_QUERY_HEADS // LOCAL_KEY_HEADS
    compact = value_weights.astype(jnp.bfloat16)
    inv_root = 1.0 / math.sqrt(D)
    score_scale = 1.0 / math.sqrt(HEAD_SIZE)
    cot_scale = math.sqrt(D / RTOK)
    causal = jnp.arange(DEVICE_TOKENS)[:, None] >= jnp.arange(DEVICE_TOKENS)[None, :]

    def replica(running, inputs):
        block_tokens, block_query_rows, block_key_rows, block_target_rows, first_old, second_old = inputs
        value_result = (jnp.dot(block_tokens, compact, preferred_element_type=jnp.float32) * inv_root).astype(jnp.bfloat16)
        query_head_count = block_query_rows.reshape(N_FSDP, DEVICE_TOKENS, LOCAL_KEY_HEADS, heads_per_group, HEAD_SIZE).astype(jnp.float32)
        key_head_count = block_key_rows.reshape(N_FSDP, DEVICE_TOKENS, LOCAL_KEY_HEADS, HEAD_SIZE).astype(jnp.float32)
        value_head_count = value_result.reshape(N_FSDP, DEVICE_TOKENS, LOCAL_KEY_HEADS, HEAD_SIZE).astype(jnp.float32)
        scores = jnp.einsum('btgjd,bsgd->bgjts', query_head_count, key_head_count) * score_scale
        scores = jnp.where(causal, scores, -jnp.inf)
        row_top = lax.optimization_barrier(jnp.max(scores, axis=-1, keepdims=True))
        expo = jnp.exp(scores - row_top)
        probs = (expo / lax.optimization_barrier(jnp.sum(expo, axis=-1, keepdims=True))).astype(jnp.bfloat16)
        outputs = jnp.einsum('bgjts,bsgd->btgjd', probs.astype(jnp.float32), value_head_count)
        objective = block_target_rows.reshape(N_FSDP, DEVICE_TOKENS, LOCAL_KEY_HEADS, heads_per_group, HEAD_SIZE).astype(jnp.float32)
        residual_term = ((outputs - objective) * cot_scale).astype(jnp.bfloat16)
        value_grad = jnp.einsum('bgjts,btgjd->bsgd', probs.astype(jnp.float32), residual_term.astype(jnp.float32))
        value_grad = value_grad.astype(jnp.bfloat16).reshape(N_FSDP, DEVICE_TOKENS, KVW)
        partial_value = jnp.einsum('bsi,bsc->bic', block_tokens.reshape(N_FSDP, DEVICE_TOKENS, D).astype(jnp.float32), value_grad.astype(jnp.float32))
        partial_value = lax.optimization_barrier(partial_value.astype(jnp.bfloat16))
        gradient = lax.optimization_barrier(jnp.sum(partial_value.astype(jnp.float32), axis=0)) * inv_root
        first_new = first_decay * first_old + (1.0 - first_decay) * gradient
        second_new = second_decay * second_old + (1.0 - second_decay) * gradient * gradient
        direction = first_new / (jnp.sqrt(second_new) + epsilon) + weight_decay * value_weights
        return (running + direction, None)
    total, _ = lax.scan(replica, jnp.zeros((D, KVW), value_weights.dtype), (tokens.reshape(N_REP, RTOK, D), queries.reshape(N_REP, RTOK, QW), rotated_key_rows.reshape(N_REP, RTOK, KVW), targets.reshape(N_REP, RTOK, QW), first_moment, second_moment))
    mean_direction = total / N_REP
    new_momentum = momentum_keep * momentum + mean_direction
    new_weights = value_weights - outer_rate * inner_rate * (mean_direction + momentum_keep * new_momentum)
    return (new_weights, new_momentum)
```

```python
import functools
import math

import jax
import jax.numpy as jnp
from jax import lax
from jax.experimental import pallas as pl
from jax.experimental.pallas import tpu as pltpu
from jax.sharding import PartitionSpec as P

D = 4096
HEAD_SIZE = 128


first_decay = 0.9
second_decay = 0.95
weight_decay = 0.1
inner_rate = 0.05
outer_rate = 0.7
momentum_keep = 0.9
epsilon = 1e-08

BF = jnp.bfloat16
F32 = jnp.float32
VMEM = pl.BlockSpec(memory_space=pltpu.VMEM)
PARAMS = pltpu.CompilerParams(vmem_limit_bytes=48 * 1024 * 1024)


def cost(flops, nbytes):
    return pl.CostEstimate(flops=flops, bytes_accessed=nbytes, transcendentals=0)


def dot(a, b, dims=((1,), (0,))):
    return lax.dot_general(a, b, (dims, ((), ())), preferred_element_type=F32)


def attention_kernel(groups, per_group, queries, keys, targets, g_hi, g_lo, cross):
    seq = queries.shape[0]
    wide = per_group * seq
    source = lax.broadcasted_iota(jnp.int32, (seq, wide), 0)
    reader = lax.rem(lax.broadcasted_iota(jnp.int32, (seq, wide), 1), seq)
    causal = source <= reader
    for g in range(groups):
        cols = slice(g * HEAD_SIZE, (g + 1) * HEAD_SIZE)
        heads = [
            slice((g * per_group + h) * HEAD_SIZE, (g * per_group + h + 1) * HEAD_SIZE)
            for h in range(per_group)
        ]
        query = jnp.concatenate([queries[:, h] for h in heads], axis=0)
        target = jnp.concatenate([targets[:, h] for h in heads], axis=0)
        scores = dot(keys[:, cols], query, ((1,), (1,))) * (1.0 / math.sqrt(HEAD_SIZE))
        scores = jnp.where(causal, scores, -jnp.inf)
        expo = jnp.exp(scores - jnp.max(scores, axis=0, keepdims=True))
        probs = (expo / jnp.sum(expo, axis=0, keepdims=True)).astype(BF)
        gram = dot(probs, probs, ((1,), (1,)))
        high = gram.astype(BF)
        g_hi[:, cols] = high
        g_lo[:, cols] = (gram - high.astype(F32)).astype(BF)
        cross[:, cols] = dot(probs, target)


def own_kernel(tokens, weights, compact, own):
    compact[...] = weights[...].astype(BF)
    own[...] = dot(tokens[...], compact[...])


def partial_kernel(n, *refs):
    blocks, compact, outs = refs[:n], refs[n], refs[n + 1 :]
    for block, out in zip(blocks, outs):
        out[...] = dot(block[...], compact[...]).astype(BF)


def transpose_kernel(n, *refs):
    blocks, out = refs[:n], refs[n]
    seq = blocks[0].shape[0]
    for k, block in enumerate(blocks):
        out[:, k * seq : (k + 1) * seq] = block[...].T


def value_grad_kernel(n, scale, *refs):
    own, parts = refs[0], refs[1:n]
    g_hi, g_lo, cross, out = refs[n:]
    total = own[...]
    for part in parts:
        total = total + part[...].astype(F32)
    value = (total * (1.0 / math.sqrt(D))).astype(BF)
    for g in range(out.shape[1] // HEAD_SIZE):
        cols = slice(g * HEAD_SIZE, (g + 1) * HEAD_SIZE)
        acc = dot(g_hi[:, cols], value[:, cols]) + dot(g_lo[:, cols], value[:, cols])
        out[:, cols] = ((acc - cross[:, cols]) * scale).astype(BF)


def direction_kernel(n, start, features, *refs):
    grads = refs[:n]
    first, second, weights, out, stacked = refs[n:]
    seq = grads[0].shape[0]

    @pl.when(pl.program_id(0) == 0)
    def _():
        for k, grad in enumerate(grads):
            stacked[k * seq : (k + 1) * seq, :] = grad[...]

    gradient = dot(features[...], stacked[...]) * (1.0 / math.sqrt(D))
    first_new = first_decay * first[0] + (1.0 - first_decay) * gradient
    second_new = second_decay * second[0] + (1.0 - second_decay) * gradient * gradient
    direction = first_new / (jnp.sqrt(second_new) + epsilon) + weight_decay * weights[...]
    out[...] = direction.astype(out.dtype)


def direction_half(start, count, block, features, grads, first, second, weights, dtype):
    n = len(grads)
    width = weights.shape[1]
    seqs = features.shape[1]
    full = pl.BlockSpec((grads[0].shape[0], width), lambda i, s: (0, 0))
    moment = pl.BlockSpec((1, block, width), lambda i, s: (0, s[0] + i, 0))
    rows = count * block
    return pl.pallas_call(
        functools.partial(direction_kernel, n),
        grid_spec=pltpu.PrefetchScalarGridSpec(
            num_scalar_prefetch=1,
            grid=(count,),
            in_specs=[pl.BlockSpec((block, seqs), lambda i, s: (s[0] + i, 0))]
            + [full] * n
            + [moment, moment, pl.BlockSpec((block, width), lambda i, s: (s[0] + i, 0))],
            out_specs=pl.BlockSpec((block, width), lambda i, s: (i, 0)),
            scratch_shapes=[pltpu.VMEM((seqs, width), BF)],
        ),
        out_shape=jax.ShapeDtypeStruct((rows, width), dtype),
        compiler_params=PARAMS,
        cost_estimate=cost(2 * rows * seqs * width, rows * width * 16),
        name="direction",
    )(start, features, *grads, first, second, weights)


def split_kernel(n, where, mine, theirs, own, *outs):
    rows = own.shape[0]
    for k in range(n):
        at = pl.ds(pl.multiple_of((where[0] ^ k) * rows, rows), rows)
        total = mine[at, :] + theirs[at, :].astype(F32)
        if k == 0:
            own[...] = total
        else:
            outs[k - 1][...] = total.astype(BF)


def mean_kernel(inv, own, *refs):
    parts, out = refs[:-1], refs[-1]
    total = own[...]
    for part in parts:
        total = total + part[...].astype(F32)
    out[...] = (total * inv).astype(BF)


def outer_kernel(mean, momentum, weights, new_weights, new_momentum):
    mean_direction = mean[...].astype(F32)
    kept = momentum_keep * momentum[...] + mean_direction
    new_momentum[...] = kept
    new_weights[...] = weights[...] - outer_rate * inner_rate * (
        mean_direction + momentum_keep * kept
    )


def partner(i, k, n):
    return i ^ k if n & (n - 1) == 0 else (i + k) % n


def exchange(x, axis, k):
    n = lax.axis_size(axis)
    return lax.ppermute(x, axis, [(i, partner(i, k, n)) for i in range(n)])


def per_device(
    tokens, queries, rotated_key_rows, targets, value_weights, momentum, first_moment, second_moment
):
    seq_len = tokens.shape[0]
    rows, width = value_weights.shape
    n_seq = lax.axis_size("fsdp")
    n_rep = lax.axis_size("rep")
    groups = rotated_key_rows.shape[1] // HEAD_SIZE
    heads_per_group = queries.shape[1] // rotated_key_rows.shape[1]
    cot_scale = math.sqrt(D / (seq_len * n_seq))
    me = lax.axis_index("fsdp")
    hops = range(1, n_seq)
    power = n_seq & (n_seq - 1) == 0

    def columns(k):
        at = me ^ k if power else lax.rem(me + k, n_seq)
        return lax.dynamic_slice(tokens, (0, at * rows), (seq_len, rows))

    def sender(k):
        return k if power or k == 0 else n_seq - k

    own_block = columns(0)
    blocks = [exchange(columns(k), "fsdp", k) for k in hops]

    block_shape = jax.ShapeDtypeStruct((seq_len, width), BF)
    wide_shape = jax.ShapeDtypeStruct((seq_len, width), F32)
    g_hi, g_lo, cross = pl.pallas_call(
        functools.partial(attention_kernel, groups, heads_per_group),
        out_shape=(block_shape, block_shape, wide_shape),
        in_specs=[VMEM] * 3,
        out_specs=(VMEM,) * 3,
        compiler_params=PARAMS,
        cost_estimate=cost(6 * seq_len * seq_len * queries.shape[1], 4 * queries.size),
        name="attention",
    )(queries, rotated_key_rows, targets)
    compact, own_value = pl.pallas_call(
        own_kernel,
        out_shape=(jax.ShapeDtypeStruct((rows, width), BF), wide_shape),
        in_specs=[VMEM] * 2,
        out_specs=(VMEM,) * 2,
        compiler_params=PARAMS,
        cost_estimate=cost(2 * seq_len * rows * width, 6 * rows * width),
        name="own_value",
    )(own_block, value_weights)

    products = pl.pallas_call(
        functools.partial(partial_kernel, n_seq - 1),
        out_shape=(block_shape,) * (n_seq - 1),
        in_specs=[VMEM] * n_seq,
        out_specs=(VMEM,) * (n_seq - 1),
        compiler_params=PARAMS,
        cost_estimate=cost(2 * seq_len * rows * width * (n_seq - 1), 2 * rows * width),
        name="partial_values",
    )(*blocks, compact)
    parts = [exchange(products[k - 1], "fsdp", sender(k)) for k in hops]
    features = pl.pallas_call(
        functools.partial(transpose_kernel, n_seq),
        out_shape=jax.ShapeDtypeStruct((rows, n_seq * seq_len), BF),
        in_specs=[VMEM] * n_seq,
        out_specs=VMEM,
        compiler_params=PARAMS,
        cost_estimate=cost(0, 4 * rows * n_seq * seq_len),
        name="transpose_tokens",
    )(own_block, *blocks)
    value_grad = pl.pallas_call(
        functools.partial(value_grad_kernel, n_seq, cot_scale),
        out_shape=block_shape,
        in_specs=[VMEM] * (n_seq + 3),
        out_specs=VMEM,
        compiler_params=PARAMS,
        cost_estimate=cost(4 * seq_len * seq_len * width, 20 * seq_len * width),
        name="value_grad",
    )(own_value, *parts, g_hi, g_lo, cross)
    grads = [value_grad] + [exchange(value_grad, "fsdp", k) for k in hops]

    here = lax.axis_index("rep")
    if n_rep == 8 and rows % 64 == 0:
        core = lax.rem(here, 2)
        chip = here // 2
        half = rows // 2
        piece = rows // 8
        count = 2
        block = half // count
        args = (features, grads, first_moment, second_moment, value_weights)
        theirs = direction_half(jnp.reshape((1 - core) * count, (1,)), count, block, *args, BF)
        arrived = exchange(theirs, "rep", 1)
        mine = direction_half(jnp.reshape(core * count, (1,)), count, block, *args, F32)
        small = jax.ShapeDtypeStruct((piece, width), BF)
        own, *sends = pl.pallas_call(
            functools.partial(split_kernel, 4),
            out_shape=(jax.ShapeDtypeStruct((piece, width), F32),) + (small,) * 3,
            in_specs=[pl.BlockSpec(memory_space=pltpu.SMEM), VMEM, VMEM],
            out_specs=(VMEM,) * 4,
            compiler_params=PARAMS,
            cost_estimate=cost(0, 10 * half * width),
            name="chip_sum",
        )(jnp.reshape(chip, (1,)), mine, arrived)
        got = [exchange(s, "rep", 2 * k) for k, s in zip((1, 2, 3), sends)]
        mean = pl.pallas_call(
            functools.partial(mean_kernel, 1.0 / n_rep),
            out_shape=small,
            in_specs=[VMEM] * 4,
            out_specs=VMEM,
            compiler_params=PARAMS,
            cost_estimate=cost(0, 10 * piece * width),
            name="mean_direction",
        )(own, *got)
        pieces = [mean] + [exchange(mean, "rep", 2 * k) for k in (1, 2, 3)]
        ordered = jnp.zeros((4, piece, width), BF)
        for k, p in enumerate(pieces):
            ordered = lax.dynamic_update_slice(ordered, p[None], (chip ^ k, 0, 0))
        ordered = ordered.reshape(half, width)
        other = exchange(ordered, "rep", 1)
        low = jnp.where(core == 0, ordered, other)
        high = jnp.where(core == 0, other, ordered)
        mean_direction = jnp.concatenate([low, high], axis=0)
    else:
        direction = direction_half(
            jnp.zeros((1,), jnp.int32), 2, rows // 2, features, grads, first_moment, second_moment,
            value_weights, F32,
        )
        mean_direction = lax.psum(direction, "rep") / n_rep

    count = 4
    blocked = pl.BlockSpec((rows // count, width), lambda i: (i, 0))
    full_shape = jax.ShapeDtypeStruct((rows, width), F32)
    new_weights, new_momentum = pl.pallas_call(
        outer_kernel,
        grid=(count,),
        out_shape=(full_shape, full_shape),
        in_specs=[blocked] * 3,
        out_specs=(blocked, blocked),
        compiler_params=PARAMS,
        cost_estimate=cost(0, 18 * rows * width),
        name="outer_step",
    )(mean_direction, momentum, value_weights)
    return (new_weights, new_momentum)


def solution(mesh):
    in_specs = (
        P(("rep", "fsdp"), None),
        P(("rep", "fsdp"), None),
        P(("rep", "fsdp"), None),
        P(("rep", "fsdp"), None),
        P("fsdp", None),
        P("fsdp", None),
        P("rep", "fsdp", None),
        P("rep", "fsdp", None),
    )
    out_specs = (P("fsdp", None), P("fsdp", None))
    return jax.shard_map(
        per_device, mesh=mesh, in_specs=in_specs, out_specs=out_specs, check_vma=False
    )
```

```python
import functools
import math

import jax
import jax.numpy as jnp
from jax import lax
from jax.experimental import pallas as pl
from jax.experimental.pallas import tpu as pltpu
from jax.sharding import PartitionSpec as P

D = 4096
HEAD_SIZE = 128


first_decay = 0.9
second_decay = 0.95
weight_decay = 0.1
inner_rate = 0.05
outer_rate = 0.7
momentum_keep = 0.9
epsilon = 1e-08

BF = jnp.bfloat16
F32 = jnp.float32
VMEM = pl.BlockSpec(memory_space=pltpu.VMEM)
ANY = pl.BlockSpec(memory_space=pl.ANY)
SMEM = pl.BlockSpec(memory_space=pltpu.SMEM)
PARAMS = pltpu.CompilerParams(vmem_limit_bytes=12 * 1024 * 1024)


def cost(flops, nbytes):
    return pl.CostEstimate(flops=flops, bytes_accessed=nbytes, transcendentals=0)


def dot(a, b, dims=((1,), (0,))):
    return lax.dot_general(a, b, (dims, ((), ())), preferred_element_type=F32)


def attention_kernel(groups, per_group, queries, keys, targets, g_hi, g_lo, cross):
    seq = queries.shape[0]
    wide = per_group * seq
    source = lax.broadcasted_iota(jnp.int32, (seq, wide), 0)
    reader = lax.rem(lax.broadcasted_iota(jnp.int32, (seq, wide), 1), seq)
    causal = source <= reader
    for g in range(groups):
        cols = slice(g * HEAD_SIZE, (g + 1) * HEAD_SIZE)
        heads = [
            slice((g * per_group + h) * HEAD_SIZE, (g * per_group + h + 1) * HEAD_SIZE)
            for h in range(per_group)
        ]
        query = jnp.concatenate([queries[:, h] for h in heads], axis=0)
        target = jnp.concatenate([targets[:, h] for h in heads], axis=0)
        scores = dot(keys[:, cols], query, ((1,), (1,))) * (1.0 / math.sqrt(HEAD_SIZE))
        scores = jnp.where(causal, scores, -jnp.inf)
        expo = jnp.exp(scores - jnp.max(scores, axis=0, keepdims=True))
        probs = (expo / jnp.sum(expo, axis=0, keepdims=True)).astype(BF)
        gram = dot(probs, probs, ((1,), (1,)))
        high = gram.astype(BF)
        g_hi[:, cols] = high
        g_lo[:, cols] = (gram - high.astype(F32)).astype(BF)
        cross[:, cols] = dot(probs, target)


def own_kernel(tokens, weights, compact, own):
    compact[...] = weights[...].astype(BF)
    own[...] = dot(tokens[...], compact[...])


def partial_kernel(n, *refs):
    blocks, compact, outs = refs[:n], refs[n], refs[n + 1 :]
    for block, out in zip(blocks, outs):
        out[...] = dot(block[...], compact[...]).astype(BF)


def transpose_kernel(n, *refs):
    blocks, out = refs[:n], refs[n]
    seq = blocks[0].shape[0]
    for k, block in enumerate(blocks):
        out[:, k * seq : (k + 1) * seq] = block[...].T


def local(kernel, shapes, *args, flops=0, name):
    specs = [SMEM if a.dtype == jnp.int32 else VMEM for a in args]
    nbytes = sum(a.size * a.dtype.itemsize for a in (*args, *shapes))
    return pl.pallas_call(
        kernel,
        out_shape=tuple(shapes),
        in_specs=specs,
        out_specs=(VMEM,) * len(shapes),
        compiler_params=PARAMS,
        cost_estimate=cost(flops, nbytes),
        name=name,
    )(*args)


def after(values, *first):
    return lax.optimization_barrier((values, first))[0]


def to_chips(sends):
    return [exchange(s, "rep", 2 * k) for k, s in zip((1, 2, 3), sends)]


def value_grad_kernel(n, scale, *refs):
    own, parts = refs[0], refs[1:n]
    g_hi, g_lo, cross, out = refs[n:]
    total = own[...]
    for part in parts:
        total = total + part[...].astype(F32)
    value = (total * (1.0 / math.sqrt(D))).astype(BF)
    for g in range(out.shape[1] // HEAD_SIZE):
        cols = slice(g * HEAD_SIZE, (g + 1) * HEAD_SIZE)
        acc = dot(g_hi[:, cols], value[:, cols]) + dot(g_lo[:, cols], value[:, cols])
        out[:, cols] = ((acc - cross[:, cols]) * scale).astype(BF)


def direction_of(features, stacked, first, second, weights, at):
    summed = dot(features[at, :], stacked)
    first_new = first_decay * first[0, at, :] + (1.0 - first_decay) / math.sqrt(D) * summed
    second_new = second_decay * second[0, at, :] + (1.0 - second_decay) / D * summed * summed
    return first_new / (jnp.sqrt(second_new) + epsilon) + weight_decay * weights[at, :]


def rows_at(start, count):
    return pl.ds(pl.multiple_of(start, count), count)


def first_row(ids, other, offset, half):
    core = lax.rem(ids[1], 2)
    return (1 - core if other else core) * half + offset


def half_kernel(n, rows, other, ids, features, *refs):
    grads = refs[:n]
    first, second, weights, out = refs[n:]
    stacked = jnp.concatenate([g[...] for g in grads], axis=0)
    start = first_row(ids, other, 0, weights.shape[0] // 2)
    for i in range(0, out.shape[0], rows):
        at = rows_at(start + i, rows)
        total = direction_of(features, stacked, first, second, weights, at)
        out[i : i + rows, :] = total.astype(out.dtype)


def split_kernel(ids, mine, theirs, own, *outs):
    rows = own.shape[0]
    for k in range(len(outs) + 1):
        at = rows_at((ids[1] // 2 ^ k) * rows, rows)
        total = mine[at, :] + theirs[at, :].astype(F32)
        if k == 0:
            own[...] = total
        else:
            outs[k - 1][...] = total.astype(BF)


def direction_kernel(n, features, *refs):
    grads = refs[:n]
    first, second, weights, out = refs[n:]
    stacked = jnp.concatenate([g[...] for g in grads], axis=0)
    out[...] = direction_of(features, stacked, first, second, weights, slice(None))


def mean_kernel(inv, own, *refs):
    parts, out = refs[:-1], refs[-1]
    total = own[...]
    for part in parts:
        total = total + part[...].astype(F32)
    out[...] = (total * inv).astype(BF)


def outer_kernel(mean, momentum, weights, new_weights, new_momentum):
    mean_direction = mean[...].astype(F32)
    kept = momentum_keep * momentum[...] + mean_direction
    new_momentum[...] = kept
    new_weights[...] = weights[...] - outer_rate * inner_rate * (
        mean_direction + momentum_keep * kept
    )


def stack_kernel(*refs):
    pieces, out = refs[:-1], refs[-1]
    rows = pieces[0].shape[0]
    for k, piece in enumerate(pieces):
        out[k * rows : (k + 1) * rows, :] = piece[...]


def piece_kernel(n, other, offset, ids, *refs):
    means = refs[:n]
    momentum, weights = refs[n : n + 2]
    new_weights, new_momentum, w_out, m_out, sems = refs[-5:]
    rows = w_out.shape[1]
    start = first_row(ids, other, offset, weights.shape[0] // 2)
    copies = []
    for k in range(4):
        mean = means[k] if n == 4 else means[0].at[k * rows : (k + 1) * rows, :]
        at = rows_at(start + (ids[1] // 2 ^ k) * rows, rows)
        outer_kernel(mean, momentum.at[at, :], weights.at[at, :], w_out.at[k], m_out.at[k])
        for i, (src, dst) in enumerate(((w_out, new_weights), (m_out, new_momentum))):
            copy = pltpu.make_async_copy(src.at[k], dst.at[at, :], sems.at[i, k])
            copy.start()
            copies.append(copy)
    for copy in copies:
        copy.wait()


def outer_piece(ids, other, offset, means, momentum, weights, outs):
    n = len(means)
    width = weights.shape[1]
    piece = means[0].shape[0] * n // 4
    full_shape = jax.ShapeDtypeStruct(weights.shape, F32)
    return pl.pallas_call(
        functools.partial(piece_kernel, n, other, offset),
        out_shape=(full_shape, full_shape),
        in_specs=[SMEM] + [VMEM] * (n + 2) + [ANY] * len(outs),
        out_specs=(ANY, ANY),
        scratch_shapes=[pltpu.VMEM((4, piece, width), F32)] * 2
        + [pltpu.SemaphoreType.DMA((2, 4))],
        input_output_aliases={n + 3 + i: i for i in range(len(outs))},
        compiler_params=PARAMS,
        cost_estimate=cost(0, 72 * piece * width),
        name="outer_step",
    )(ids, *means, momentum, weights, *outs)


def partner(i, k, n):
    return i ^ k if n & (n - 1) == 0 else (i + k) % n


def exchange(x, axis, k):
    n = lax.axis_size(axis)
    return lax.ppermute(x, axis, [(i, partner(i, k, n)) for i in range(n)])


def per_device(
    tokens, queries, rotated_key_rows, targets, value_weights, momentum, first_moment, second_moment
):
    seq_len = tokens.shape[0]
    rows, width = value_weights.shape
    n_seq = lax.axis_size("fsdp")
    n_rep = lax.axis_size("rep")
    groups = rotated_key_rows.shape[1] // HEAD_SIZE
    heads_per_group = queries.shape[1] // rotated_key_rows.shape[1]
    cot_scale = math.sqrt(D / (seq_len * n_seq))
    ids = jnp.stack([lax.axis_index("fsdp"), lax.axis_index("rep")]).astype(jnp.int32)
    ids, tokens = lax.optimization_barrier((ids, tokens))
    hops = tuple(range(n_seq - 1, 0, -1))
    power = n_seq & (n_seq - 1) == 0

    def sender(k):
        return k if power or k == 0 else n_seq - k

    def columns(k):
        block = ids[0] ^ k if power else lax.rem(ids[0] + k, n_seq)
        return lax.dynamic_slice(tokens, (0, block * rows), (seq_len, rows))

    own_block = columns(0)
    blocks = [exchange(columns(k), "fsdp", k) for k in hops]

    block_shape = jax.ShapeDtypeStruct((seq_len, width), BF)
    wide_shape = jax.ShapeDtypeStruct((seq_len, width), F32)
    g_hi, g_lo, cross = pl.pallas_call(
        functools.partial(attention_kernel, groups, heads_per_group),
        out_shape=(block_shape, block_shape, wide_shape),
        in_specs=[VMEM] * 3,
        out_specs=(VMEM,) * 3,
        compiler_params=PARAMS,
        cost_estimate=cost(6 * seq_len * seq_len * queries.shape[1], 4 * queries.size),
        name="attention",
    )(queries, rotated_key_rows, targets)
    compact, own_value = pl.pallas_call(
        own_kernel,
        out_shape=(jax.ShapeDtypeStruct((rows, width), BF), wide_shape),
        in_specs=[VMEM] * 2,
        out_specs=(VMEM,) * 2,
        compiler_params=PARAMS,
        cost_estimate=cost(2 * seq_len * rows * width, 6 * rows * width),
        name="own_value",
    )(own_block, value_weights)

    products = pl.pallas_call(
        functools.partial(partial_kernel, n_seq - 1),
        out_shape=(block_shape,) * (n_seq - 1),
        in_specs=[VMEM] * n_seq,
        out_specs=(VMEM,) * (n_seq - 1),
        compiler_params=PARAMS,
        cost_estimate=cost(2 * seq_len * rows * width * (n_seq - 1), 2 * rows * width),
        name="partial_values",
    )(*blocks, compact)
    parts = [exchange(p, "fsdp", sender(k)) for k, p in zip(hops, products)]
    features = pl.pallas_call(
        functools.partial(transpose_kernel, n_seq),
        out_shape=jax.ShapeDtypeStruct((rows, n_seq * seq_len), BF),
        in_specs=[VMEM] * n_seq,
        out_specs=VMEM,
        compiler_params=PARAMS,
        cost_estimate=cost(0, 4 * rows * n_seq * seq_len),
        name="transpose_tokens",
    )(own_block, *blocks)
    value_grad = pl.pallas_call(
        functools.partial(value_grad_kernel, n_seq, cot_scale),
        out_shape=block_shape,
        in_specs=[VMEM] * (n_seq + 3),
        out_specs=VMEM,
        compiler_params=PARAMS,
        cost_estimate=cost(4 * seq_len * seq_len * width, 20 * seq_len * width),
        name="value_grad",
    )(own_value, *parts, g_hi, g_lo, cross)
    grads = [value_grad] + [exchange(value_grad, "fsdp", k) for k in hops]

    moments = (first_moment, second_moment, value_weights)
    n = n_seq
    if n_rep != 8 or rows % 128:
        direction = pl.pallas_call(
            functools.partial(direction_kernel, n),
            out_shape=jax.ShapeDtypeStruct((rows, width), F32),
            in_specs=[VMEM] * (n + 4),
            out_specs=VMEM,
            compiler_params=PARAMS,
            name="direction",
        )(features, *grads, *moments)
        full_shape = jax.ShapeDtypeStruct((rows, width), F32)
        return pl.pallas_call(
            outer_kernel,
            out_shape=(full_shape, full_shape),
            in_specs=[VMEM] * 3,
            out_specs=(VMEM, VMEM),
            compiler_params=PARAMS,
            name="outer_step",
        )(lax.psum(direction, "rep") / n_rep, momentum, value_weights)

    half = rows // 2
    piece = half // 4
    small = jax.ShapeDtypeStruct((piece, width), BF)

    def half_direction(other, dtype):
        return local(
            functools.partial(half_kernel, n, min(half, 128), other),
            (jax.ShapeDtypeStruct((half, width), dtype),),
            ids, features, *grads, *moments,
            flops=2 * half * width * features.shape[1],
            name="direction",
        )[0]

    theirs = half_direction(True, BF)
    arrived = exchange(theirs, "rep", 1)
    mine = half_direction(False, F32)
    own, *sends = local(
        split_kernel, (jax.ShapeDtypeStruct((piece, width), F32),) + (small,) * 3,
        ids, mine, arrived, name="chip_sum",
    )
    got = to_chips(sends)
    mean = local(
        functools.partial(mean_kernel, 1.0 / n_rep), (small,), own, *got, name="mean_direction"
    )[0]
    means = [mean] + to_chips([mean] * 3)
    stack = local(stack_kernel, (jax.ShapeDtypeStruct((half, width), BF),), *means, name="stack")[0]
    other = exchange(stack, "rep", 1)
    outs = outer_piece(ids, False, 0, means, momentum, value_weights, ())
    outs = outer_piece(ids, True, 0, [other], momentum, value_weights, outs)
    return tuple(outs)


def solution(mesh):
    in_specs = (
        P(("rep", "fsdp"), None),
        P(("rep", "fsdp"), None),
        P(("rep", "fsdp"), None),
        P(("rep", "fsdp"), None),
        P("fsdp", None),
        P("fsdp", None),
        P("rep", "fsdp", None),
        P("rep", "fsdp", None),
    )
    out_specs = (P("fsdp", None), P("fsdp", None))
    return jax.shard_map(
        per_device, mesh=mesh, in_specs=in_specs, out_specs=out_specs, check_vma=False
    )
```

```python
import functools
import math

import jax
import jax.numpy as jnp
from jax import lax
from jax.experimental import pallas as pl
from jax.experimental.pallas import tpu as pltpu
from jax.sharding import PartitionSpec as P

D = 4096
HEAD_SIZE = 128


first_decay = 0.9
second_decay = 0.95
weight_decay = 0.1
inner_rate = 0.05
outer_rate = 0.7
momentum_keep = 0.9
epsilon = 1e-08

BF = jnp.bfloat16
F32 = jnp.float32
VMEM = pl.BlockSpec(memory_space=pltpu.VMEM)
ANY = pl.BlockSpec(memory_space=pl.ANY)
PARAMS = pltpu.CompilerParams(vmem_limit_bytes=12 * 1024 * 1024)


def cost(flops, nbytes):
    return pl.CostEstimate(flops=flops, bytes_accessed=nbytes, transcendentals=0)


def dot(a, b, dims=((1,), (0,))):
    return lax.dot_general(a, b, (dims, ((), ())), preferred_element_type=F32)


def attention_kernel(groups, per_group, queries, keys, targets, g_hi, g_lo, cross):
    seq = queries.shape[0]
    wide = per_group * seq
    source = lax.broadcasted_iota(jnp.int32, (seq, wide), 0)
    reader = lax.rem(lax.broadcasted_iota(jnp.int32, (seq, wide), 1), seq)
    causal = source <= reader
    for g in range(groups):
        cols = slice(g * HEAD_SIZE, (g + 1) * HEAD_SIZE)
        heads = [
            slice((g * per_group + h) * HEAD_SIZE, (g * per_group + h + 1) * HEAD_SIZE)
            for h in range(per_group)
        ]
        query = jnp.concatenate([queries[:, h] for h in heads], axis=0)
        target = jnp.concatenate([targets[:, h] for h in heads], axis=0)
        scores = dot(keys[:, cols], query, ((1,), (1,))) * (1.0 / math.sqrt(HEAD_SIZE))
        scores = jnp.where(causal, scores, -jnp.inf)
        expo = jnp.exp(scores - jnp.max(scores, axis=0, keepdims=True))
        probs = (expo / jnp.sum(expo, axis=0, keepdims=True)).astype(BF)
        gram = dot(probs, probs, ((1,), (1,)))
        high = gram.astype(BF)
        g_hi[:, cols] = high
        g_lo[:, cols] = (gram - high.astype(F32)).astype(BF)
        cross[:, cols] = dot(probs, target)


def own_kernel(tokens, weights, compact, own):
    compact[...] = weights[...].astype(BF)
    own[...] = dot(tokens[...], compact[...])


def partial_kernel(n, *refs):
    blocks, compact, outs = refs[:n], refs[n], refs[n + 1 :]
    for block, out in zip(blocks, outs):
        out[...] = dot(block[...], compact[...]).astype(BF)


def transpose_kernel(n, *refs):
    blocks, out = refs[:n], refs[n]
    seq = blocks[0].shape[0]
    for k, block in enumerate(blocks):
        out[:, k * seq : (k + 1) * seq] = block[...].T


def local(kernel, shapes, *args, flops=0, name):
    specs = [VMEM] * len(args)
    nbytes = sum(a.size * a.dtype.itemsize for a in (*args, *shapes))
    return pl.pallas_call(
        kernel,
        out_shape=tuple(shapes),
        in_specs=specs,
        out_specs=(VMEM,) * len(shapes),
        compiler_params=PARAMS,
        cost_estimate=cost(flops, nbytes),
        name=name,
    )(*args)


def after(values, *first):
    return lax.optimization_barrier((values, first))[0]


def to_chips(sends):
    return [exchange(s, "rep", 2 * k) for k, s in zip((1, 2, 3), sends)]


def value_grad_kernel(n, scale, *refs):
    own, parts = refs[0], refs[1:n]
    g_hi, g_lo, cross, out = refs[n:]
    total = own[...]
    for part in parts:
        total = total + part[...].astype(F32)
    value = (total * (1.0 / math.sqrt(D))).astype(BF)
    for g in range(out.shape[1] // HEAD_SIZE):
        cols = slice(g * HEAD_SIZE, (g + 1) * HEAD_SIZE)
        acc = dot(g_hi[:, cols], value[:, cols]) + dot(g_lo[:, cols], value[:, cols])
        out[:, cols] = ((acc - cross[:, cols]) * scale).astype(BF)


def direction_of(features, stacked, first, second, weights, at):
    summed = dot(features[at, :], stacked)
    first_new = first_decay * first[0, at, :] + (1.0 - first_decay) / math.sqrt(D) * summed
    second_new = second_decay * second[0, at, :] + (1.0 - second_decay) / D * summed * summed
    return first_new / (jnp.sqrt(second_new) + epsilon) + weight_decay * weights[at, :]


def rows_at(start, count):
    return pl.ds(pl.multiple_of(start, count), count)


def position():
    here = lax.axis_index("rep")
    return lax.div(here, 2), lax.rem(here, 2)


def first_row(other, half):
    _, core = position()
    return (1 - core if other else core) * half


def half_kernel(n, rows, other, features, *refs):
    grads = refs[:n]
    first, second, weights, out = refs[n:]
    stacked = jnp.concatenate([g[...] for g in grads], axis=0)
    start = first_row(other, weights.shape[0] // 2)
    for i in range(0, out.shape[0], rows):
        at = rows_at(start + i, rows)
        total = direction_of(features, stacked, first, second, weights, at)
        out[i : i + rows, :] = total.astype(out.dtype)


def split_kernel(mine, theirs, own, *outs):
    rows = own.shape[0]
    chip, _ = position()
    for k in range(len(outs) + 1):
        at = rows_at((chip ^ k) * rows, rows)
        total = mine[at, :] + theirs[at, :].astype(F32)
        if k == 0:
            own[...] = total
        else:
            outs[k - 1][...] = total.astype(BF)


def direction_kernel(n, features, *refs):
    grads = refs[:n]
    first, second, weights, out = refs[n:]
    stacked = jnp.concatenate([g[...] for g in grads], axis=0)
    out[...] = direction_of(features, stacked, first, second, weights, slice(None))


def mean_kernel(inv, own, *refs):
    parts, out = refs[:-1], refs[-1]
    total = own[...]
    for part in parts:
        total = total + part[...].astype(F32)
    out[...] = (total * inv).astype(BF)


def outer_kernel(mean, momentum, weights, new_weights, new_momentum):
    mean_direction = mean[...].astype(F32)
    kept = momentum_keep * momentum[...] + mean_direction
    new_momentum[...] = kept
    new_weights[...] = weights[...] - outer_rate * inner_rate * (
        mean_direction + momentum_keep * kept
    )


def stack_kernel(*refs):
    pieces, out = refs[:-1], refs[-1]
    rows = pieces[0].shape[0]
    for k, piece in enumerate(pieces):
        out[k * rows : (k + 1) * rows, :] = piece[...]


def piece_kernel(n, other, *refs):
    means = refs[:n]
    momentum, weights = refs[n : n + 2]
    new_weights, new_momentum, w_out, m_out, sems = refs[-5:]
    rows = w_out.shape[1]
    start = first_row(other, weights.shape[0] // 2)
    chip, _ = position()
    copies = []
    for k in range(4):
        mean = means[k] if n == 4 else means[0].at[k * rows : (k + 1) * rows, :]
        at = rows_at(start + (chip ^ k) * rows, rows)
        outer_kernel(mean, momentum.at[at, :], weights.at[at, :], w_out.at[k], m_out.at[k])
        for i, (src, dst) in enumerate(((w_out, new_weights), (m_out, new_momentum))):
            copy = pltpu.make_async_copy(src.at[k], dst.at[at, :], sems.at[i, k])
            copy.start()
            copies.append(copy)
    for copy in copies:
        copy.wait()


def outer_piece(other, means, momentum, weights, outs):
    n = len(means)
    width = weights.shape[1]
    piece = means[0].shape[0] * n // 4
    full_shape = jax.ShapeDtypeStruct(weights.shape, F32)
    return pl.pallas_call(
        functools.partial(piece_kernel, n, other),
        out_shape=(full_shape, full_shape),
        in_specs=[VMEM] * (n + 2) + [ANY] * len(outs),
        out_specs=(ANY, ANY),
        scratch_shapes=[pltpu.VMEM((4, piece, width), F32)] * 2
        + [pltpu.SemaphoreType.DMA((2, 4))],
        input_output_aliases={n + 2 + i: i for i in range(len(outs))},
        compiler_params=PARAMS,
        cost_estimate=cost(0, 72 * piece * width),
        name="outer_step",
    )(*means, momentum, weights, *outs)


def exchange(x, axis, k):
    n = lax.axis_size(axis)
    return lax.ppermute(x, axis, [(i, i ^ k) for i in range(n)])


def ring_hop(i, k, n):
    if n & (n - 1):
        return (i + k) % n
    place, shift = i, 1
    while shift < n:
        place = place ^ (place >> shift)
        shift *= 2
    place = (place + k) % n
    return place ^ (place >> 1)


def turn(x, k):
    n = lax.axis_size("fsdp")
    return lax.ppermute(x, "fsdp", [(i, ring_hop(i, k, n)) for i in range(n)])


def per_device(
    tokens, queries, rotated_key_rows, targets, value_weights, momentum, first_moment, second_moment
):
    seq_len = tokens.shape[0]
    rows, width = value_weights.shape
    n_seq = lax.axis_size("fsdp")
    n_rep = lax.axis_size("rep")
    groups = rotated_key_rows.shape[1] // HEAD_SIZE
    heads_per_group = queries.shape[1] // rotated_key_rows.shape[1]
    cot_scale = math.sqrt(D / (seq_len * n_seq))
    me, tokens = lax.optimization_barrier((lax.axis_index("fsdp"), tokens))
    hops = (n_seq // 2, *[k for k in range(n_seq - 1, 0, -1) if k != n_seq // 2])
    def columns(k):
        block = ring_hop(me, k, n_seq)
        return lax.dynamic_slice(tokens, (0, block * rows), (seq_len, rows))

    own_block = columns(0)
    blocks = [turn(columns(k), k) for k in hops]

    block_shape = jax.ShapeDtypeStruct((seq_len, width), BF)
    wide_shape = jax.ShapeDtypeStruct((seq_len, width), F32)
    g_hi, g_lo, cross = pl.pallas_call(
        functools.partial(attention_kernel, groups, heads_per_group),
        out_shape=(block_shape, block_shape, wide_shape),
        in_specs=[VMEM] * 3,
        out_specs=(VMEM,) * 3,
        compiler_params=PARAMS,
        cost_estimate=cost(6 * seq_len * seq_len * queries.shape[1], 4 * queries.size),
        name="attention",
    )(queries, rotated_key_rows, targets)
    compact, own_value = pl.pallas_call(
        own_kernel,
        out_shape=(jax.ShapeDtypeStruct((rows, width), BF), wide_shape),
        in_specs=[VMEM] * 2,
        out_specs=(VMEM,) * 2,
        compiler_params=PARAMS,
        cost_estimate=cost(2 * seq_len * rows * width, 6 * rows * width),
        name="own_value",
    )(own_block, value_weights)

    products = pl.pallas_call(
        functools.partial(partial_kernel, n_seq - 1),
        out_shape=(block_shape,) * (n_seq - 1),
        in_specs=[VMEM] * n_seq,
        out_specs=(VMEM,) * (n_seq - 1),
        compiler_params=PARAMS,
        cost_estimate=cost(2 * seq_len * rows * width * (n_seq - 1), 2 * rows * width),
        name="partial_values",
    )(*blocks, compact)
    parts = [turn(p, n_seq - k) for k, p in zip(hops, products)]
    features = pl.pallas_call(
        functools.partial(transpose_kernel, n_seq),
        out_shape=jax.ShapeDtypeStruct((rows, n_seq * seq_len), BF),
        in_specs=[VMEM] * n_seq,
        out_specs=VMEM,
        compiler_params=PARAMS,
        cost_estimate=cost(0, 4 * rows * n_seq * seq_len),
        name="transpose_tokens",
    )(own_block, *blocks)
    value_grad = pl.pallas_call(
        functools.partial(value_grad_kernel, n_seq, cot_scale),
        out_shape=block_shape,
        in_specs=[VMEM] * (n_seq + 3),
        out_specs=VMEM,
        compiler_params=PARAMS,
        cost_estimate=cost(4 * seq_len * seq_len * width, 20 * seq_len * width),
        name="value_grad",
    )(own_value, *parts, g_hi, g_lo, cross)
    grads = [value_grad] + [turn(value_grad, k) for k in hops]

    moments = (first_moment, second_moment, value_weights)
    n = n_seq
    if n_rep != 8 or rows % 128:
        direction = pl.pallas_call(
            functools.partial(direction_kernel, n),
            out_shape=jax.ShapeDtypeStruct((rows, width), F32),
            in_specs=[VMEM] * (n + 4),
            out_specs=VMEM,
            compiler_params=PARAMS,
            name="direction",
        )(features, *grads, *moments)
        full_shape = jax.ShapeDtypeStruct((rows, width), F32)
        return pl.pallas_call(
            outer_kernel,
            out_shape=(full_shape, full_shape),
            in_specs=[VMEM] * 3,
            out_specs=(VMEM, VMEM),
            compiler_params=PARAMS,
            name="outer_step",
        )(lax.psum(direction, "rep") / n_rep, momentum, value_weights)

    half = rows // 2
    piece = half // 4
    small = jax.ShapeDtypeStruct((piece, width), BF)

    def half_direction(other, dtype):
        return local(
            functools.partial(half_kernel, n, min(half, 128), other),
            (jax.ShapeDtypeStruct((half, width), dtype),),
            features, *grads, *moments,
            flops=2 * half * width * features.shape[1],
            name="direction",
        )[0]

    theirs = half_direction(True, BF)
    arrived = exchange(theirs, "rep", 1)
    mine = half_direction(False, F32)
    own, *sends = local(
        split_kernel, (jax.ShapeDtypeStruct((piece, width), F32),) + (small,) * 3,
        mine, arrived, name="chip_sum",
    )
    got = to_chips(sends)
    mean = local(
        functools.partial(mean_kernel, 1.0 / n_rep), (small,), own, *got, name="mean_direction"
    )[0]
    means = [mean] + to_chips([mean] * 3)
    stack = local(stack_kernel, (jax.ShapeDtypeStruct((half, width), BF),), *means, name="stack")[0]
    other = exchange(stack, "rep", 1)
    outs = outer_piece(False, means, momentum, value_weights, ())
    outs = outer_piece(True, [other], momentum, value_weights, outs)
    return tuple(outs)


def solution(mesh):
    in_specs = (
        P(("rep", "fsdp"), None),
        P(("rep", "fsdp"), None),
        P(("rep", "fsdp"), None),
        P(("rep", "fsdp"), None),
        P("fsdp", None),
        P("fsdp", None),
        P("rep", "fsdp", None),
        P("rep", "fsdp", None),
    )
    out_specs = (P("fsdp", None), P("fsdp", None))
    return jax.shard_map(
        per_device, mesh=mesh, in_specs=in_specs, out_specs=out_specs, check_vma=False
    )
```

```python
import functools
import math

import jax
import jax.numpy as jnp
from jax import lax
from jax.experimental import pallas as pl
from jax.experimental.pallas import tpu as pltpu
from jax.sharding import PartitionSpec as P

D = 4096
HEAD_SIZE = 128


first_decay = 0.9
second_decay = 0.95
weight_decay = 0.1
inner_rate = 0.05
outer_rate = 0.7
momentum_keep = 0.9
epsilon = 1e-08

BF = jnp.bfloat16
F32 = jnp.float32
VMEM = pl.BlockSpec(memory_space=pltpu.VMEM)
ANY = pl.BlockSpec(memory_space=pl.ANY)
PARAMS = pltpu.CompilerParams(vmem_limit_bytes=12 * 1024 * 1024)


def cost(flops, nbytes):
    return pl.CostEstimate(flops=flops, bytes_accessed=nbytes, transcendentals=0)


def dot(a, b, dims=((1,), (0,))):
    return lax.dot_general(a, b, (dims, ((), ())), preferred_element_type=F32)


def attention_kernel(groups, per_group, queries, keys, targets, g_hi, g_lo, cross):
    seq = queries.shape[0]
    wide = per_group * seq
    source = lax.broadcasted_iota(jnp.int32, (seq, wide), 0)
    reader = lax.rem(lax.broadcasted_iota(jnp.int32, (seq, wide), 1), seq)
    causal = source <= reader
    for g in range(groups):
        cols = slice(g * HEAD_SIZE, (g + 1) * HEAD_SIZE)
        heads = [
            slice((g * per_group + h) * HEAD_SIZE, (g * per_group + h + 1) * HEAD_SIZE)
            for h in range(per_group)
        ]
        query = jnp.concatenate([queries[:, h] for h in heads], axis=0)
        target = jnp.concatenate([targets[:, h] for h in heads], axis=0)
        scores = dot(keys[:, cols], query, ((1,), (1,))) * (1.0 / math.sqrt(HEAD_SIZE))
        scores = jnp.where(causal, scores, -jnp.inf)
        expo = jnp.exp(scores - jnp.max(scores, axis=0, keepdims=True))
        probs = (expo / jnp.sum(expo, axis=0, keepdims=True)).astype(BF)
        gram = dot(probs, probs, ((1,), (1,)))
        high = gram.astype(BF)
        g_hi[:, cols] = high
        g_lo[:, cols] = (gram - high.astype(F32)).astype(BF)
        cross[:, cols] = dot(probs, target)


def own_kernel(tokens, weights, compact, own):
    compact[...] = weights[...].astype(BF)
    own[...] = dot(tokens[...], compact[...])


def partial_kernel(n, *refs):
    blocks, compact, outs = refs[:n], refs[n], refs[n + 1 :]
    for block, out in zip(blocks, outs):
        out[...] = dot(block[...], compact[...]).astype(out.dtype)


def add_kernel(one, two, out):
    out[...] = (one[...] + two[...].astype(F32)).astype(out.dtype)


def transpose_kernel(n, *refs):
    blocks, out = refs[:n], refs[n]
    seq = blocks[0].shape[0]
    for k, block in enumerate(blocks):
        out[:, k * seq : (k + 1) * seq] = block[...].T


def local(kernel, shapes, *args, flops=0, name):
    specs = [VMEM] * len(args)
    nbytes = sum(a.size * a.dtype.itemsize for a in (*args, *shapes))
    return pl.pallas_call(
        kernel,
        out_shape=tuple(shapes),
        in_specs=specs,
        out_specs=(VMEM,) * len(shapes),
        compiler_params=PARAMS,
        cost_estimate=cost(flops, nbytes),
        name=name,
    )(*args)


def after(values, *first):
    return lax.optimization_barrier((values, first))[0]


def to_chips(sends):
    return [exchange(s, "rep", 2 * k) for k, s in zip((1, 2, 3), sends)]


def value_grad_kernel(n, scale, *refs):
    own, parts = refs[0], refs[1:n]
    g_hi, g_lo, cross, out = refs[n:]
    total = own[...]
    for part in parts:
        total = total + part[...].astype(F32)
    value = (total * (1.0 / math.sqrt(D))).astype(BF)
    for g in range(out.shape[1] // HEAD_SIZE):
        cols = slice(g * HEAD_SIZE, (g + 1) * HEAD_SIZE)
        acc = dot(g_hi[:, cols], value[:, cols]) + dot(g_lo[:, cols], value[:, cols])
        out[:, cols] = ((acc - cross[:, cols]) * scale).astype(BF)


def direction_of(features, stacked, first, second, weights, at):
    summed = dot(features[at, :], stacked)
    first_new = first_decay * first[0, at, :] + (1.0 - first_decay) / math.sqrt(D) * summed
    second_new = second_decay * second[0, at, :] + (1.0 - second_decay) / D * summed * summed
    return first_new / (jnp.sqrt(second_new) + epsilon) + weight_decay * weights[at, :]


def rows_at(start, count):
    return pl.ds(pl.multiple_of(start, count), count)


def position():
    here = lax.axis_index("rep")
    return lax.div(here, 2), lax.rem(here, 2)


def first_row(other, half):
    _, core = position()
    return (1 - core if other else core) * half


def half_kernel(n, rows, other, features, *refs):
    grads = refs[:n]
    first, second, weights, out = refs[n:]
    stacked = jnp.concatenate([g[...] for g in grads], axis=0)
    start = first_row(other, weights.shape[0] // 2)
    for i in range(0, out.shape[0], rows):
        at = rows_at(start + i, rows)
        total = direction_of(features, stacked, first, second, weights, at)
        out[i : i + rows, :] = total.astype(out.dtype)


def split_kernel(mine, theirs, own, *outs):
    rows = own.shape[0]
    chip, _ = position()
    for k in range(len(outs) + 1):
        at = rows_at((chip ^ k) * rows, rows)
        total = mine[at, :] + theirs[at, :].astype(F32)
        if k == 0:
            own[...] = total
        else:
            outs[k - 1][...] = total.astype(BF)


def direction_kernel(n, features, *refs):
    grads = refs[:n]
    first, second, weights, out = refs[n:]
    stacked = jnp.concatenate([g[...] for g in grads], axis=0)
    out[...] = direction_of(features, stacked, first, second, weights, slice(None))


def mean_kernel(inv, own, *refs):
    parts, out = refs[:-1], refs[-1]
    total = own[...]
    for part in parts:
        total = total + part[...].astype(F32)
    out[...] = (total * inv).astype(BF)


def outer_kernel(mean, momentum, weights, new_weights, new_momentum):
    mean_direction = mean[...].astype(F32)
    kept = momentum_keep * momentum[...] + mean_direction
    new_momentum[...] = kept
    new_weights[...] = weights[...] - outer_rate * inner_rate * (
        mean_direction + momentum_keep * kept
    )


def piece_kernel(places, *refs):
    n = len(places)
    means, (momentum, weights) = refs[:n], refs[n : n + 2]
    new_weights, new_momentum, w_out, m_out, sems = refs[-5:]
    rows = w_out.shape[1]
    chip, _ = position()
    copies = []
    for j, (k, other) in enumerate(places):
        at = rows_at(first_row(other, weights.shape[0] // 2) + (chip ^ k) * rows, rows)
        outer_kernel(means[j], momentum.at[at, :], weights.at[at, :], w_out.at[j], m_out.at[j])
        for i, (src, dst) in enumerate(((w_out, new_weights), (m_out, new_momentum))):
            copy = pltpu.make_async_copy(src.at[j], dst.at[at, :], sems.at[i, j])
            copy.start()
            copies.append(copy)
    for copy in copies:
        copy.wait()


def outer_pieces(places, means, momentum, weights, outs):
    n = len(places)
    piece, width = means[0].shape
    full_shape = jax.ShapeDtypeStruct(weights.shape, F32)
    return pl.pallas_call(
        functools.partial(piece_kernel, places),
        out_shape=(full_shape, full_shape),
        in_specs=[VMEM] * (n + 2) + [ANY] * len(outs),
        out_specs=(ANY, ANY),
        scratch_shapes=[pltpu.VMEM((n, piece, width), F32)] * 2
        + [pltpu.SemaphoreType.DMA((2, n))],
        input_output_aliases={n + 2 + i: i for i in range(len(outs))},
        compiler_params=PARAMS,
        cost_estimate=cost(0, 18 * n * piece * width),
        name="outer_step",
    )(*means, momentum, weights, *outs)


def exchange(x, axis, k):
    n = lax.axis_size(axis)
    return lax.ppermute(x, axis, [(i, i ^ k) for i in range(n)])


def ring_hop(i, k, n):
    if n & (n - 1):
        return (i + k) % n
    place, shift = i, 1
    while shift < n:
        place = place ^ (place >> shift)
        shift *= 2
    place = (place + k) % n
    return place ^ (place >> 1)


def turn(x, k):
    n = lax.axis_size("fsdp")
    return lax.ppermute(x, "fsdp", [(i, ring_hop(i, k, n)) for i in range(n)])


def per_device(
    tokens, queries, rotated_key_rows, targets, value_weights, momentum, first_moment, second_moment
):
    seq_len = tokens.shape[0]
    rows, width = value_weights.shape
    n_seq = lax.axis_size("fsdp")
    n_rep = lax.axis_size("rep")
    groups = rotated_key_rows.shape[1] // HEAD_SIZE
    heads_per_group = queries.shape[1] // rotated_key_rows.shape[1]
    cot_scale = math.sqrt(D / (seq_len * n_seq))
    me, tokens = lax.optimization_barrier((lax.axis_index("fsdp"), tokens))
    hops = (n_seq // 2, *[k for k in range(n_seq - 1, 0, -1) if k != n_seq // 2])
    def columns(k):
        block = ring_hop(me, k, n_seq)
        return lax.dynamic_slice(tokens, (0, block * rows), (seq_len, rows))

    cut = {hops[0]: columns(hops[0])}
    tokens, cut[hops[0]] = lax.optimization_barrier((tokens, cut[hops[0]]))
    cut.update({k: columns(k) for k in (0, *hops[1:])})
    own_block = cut[0]
    blocks = [turn(cut[k], k) for k in hops]

    block_shape = jax.ShapeDtypeStruct((seq_len, width), BF)
    wide_shape = jax.ShapeDtypeStruct((seq_len, width), F32)
    g_hi, g_lo, cross = pl.pallas_call(
        functools.partial(attention_kernel, groups, heads_per_group),
        out_shape=(block_shape, block_shape, wide_shape),
        in_specs=[VMEM] * 3,
        out_specs=(VMEM,) * 3,
        compiler_params=PARAMS,
        cost_estimate=cost(6 * seq_len * seq_len * queries.shape[1], 4 * queries.size),
        name="attention",
    )(queries, rotated_key_rows, targets)
    compact, own_value = pl.pallas_call(
        own_kernel,
        out_shape=(jax.ShapeDtypeStruct((rows, width), BF), wide_shape),
        in_specs=[VMEM] * 2,
        out_specs=(VMEM,) * 2,
        compiler_params=PARAMS,
        cost_estimate=cost(2 * seq_len * rows * width, 6 * rows * width),
        name="own_value",
    )(own_block, value_weights)

    def product(k, dtype):
        return local(
            functools.partial(partial_kernel, 1), (jax.ShapeDtypeStruct((seq_len, width), dtype),),
            blocks[hops.index(k)], compact,
            flops=2 * seq_len * rows * width, name="partial_value",
        )[0]

    if n_seq == 4:
        passed = turn(product(2, BF), 1)
        back = turn(product(1, BF), 3)
        joined = local(add_kernel, (block_shape,), product(3, F32), passed, name="joined_value")[0]
        parts = [turn(joined, 1), back]
    else:
        parts = [turn(product(k, BF), n_seq - k) for k in hops]
    gathered = (hops[0], *hops[:0:-1])
    features = pl.pallas_call(
        functools.partial(transpose_kernel, n_seq),
        out_shape=jax.ShapeDtypeStruct((rows, n_seq * seq_len), BF),
        in_specs=[VMEM] * n_seq,
        out_specs=VMEM,
        compiler_params=PARAMS,
        cost_estimate=cost(0, 4 * rows * n_seq * seq_len),
        name="transpose_tokens",
    )(own_block, *[blocks[hops.index(k)] for k in gathered])
    value_grad = pl.pallas_call(
        functools.partial(value_grad_kernel, 1 + len(parts), cot_scale),
        out_shape=block_shape,
        in_specs=[VMEM] * (len(parts) + 4),
        out_specs=VMEM,
        compiler_params=PARAMS,
        cost_estimate=cost(4 * seq_len * seq_len * width, 20 * seq_len * width),
        name="value_grad",
    )(own_value, *parts, g_hi, g_lo, cross)
    grads = [value_grad] + [turn(value_grad, k) for k in gathered]

    moments = (first_moment, second_moment, value_weights)
    n = n_seq
    if n_rep != 8 or rows % 128:
        direction = pl.pallas_call(
            functools.partial(direction_kernel, n),
            out_shape=jax.ShapeDtypeStruct((rows, width), F32),
            in_specs=[VMEM] * (n + 4),
            out_specs=VMEM,
            compiler_params=PARAMS,
            name="direction",
        )(features, *grads, *moments)
        full_shape = jax.ShapeDtypeStruct((rows, width), F32)
        return pl.pallas_call(
            outer_kernel,
            out_shape=(full_shape, full_shape),
            in_specs=[VMEM] * 3,
            out_specs=(VMEM, VMEM),
            compiler_params=PARAMS,
            name="outer_step",
        )(lax.psum(direction, "rep") / n_rep, momentum, value_weights)

    half = rows // 2
    piece = half // 4
    small = jax.ShapeDtypeStruct((piece, width), BF)

    def half_direction(other, dtype):
        return local(
            functools.partial(half_kernel, n, min(half, 128), other),
            (jax.ShapeDtypeStruct((half, width), dtype),),
            features, *grads, *moments,
            flops=2 * half * width * features.shape[1],
            name="direction",
        )[0]

    theirs = half_direction(True, BF)
    arrived = exchange(theirs, "rep", 1)
    mine = half_direction(False, F32)
    own, *sends = local(
        split_kernel, (jax.ShapeDtypeStruct((piece, width), F32),) + (small,) * 3,
        mine, arrived, name="chip_sum",
    )
    got = to_chips(sends)
    mean = local(
        functools.partial(mean_kernel, 1.0 / n_rep), (small,), own, *got, name="mean_direction"
    )[0]
    got = to_chips([mean] * 3)
    theirs = [exchange(g, "rep", 1) for g in (mean, *got)]
    outs = outer_pieces(
        tuple((k, False) for k in range(4)), [mean, *got], momentum, value_weights, ()
    )
    return tuple(
        outer_pieces(tuple((k, True) for k in range(4)), theirs, momentum, value_weights, outs)
    )


def solution(mesh):
    in_specs = (
        P(("rep", "fsdp"), None),
        P(("rep", "fsdp"), None),
        P(("rep", "fsdp"), None),
        P(("rep", "fsdp"), None),
        P("fsdp", None),
        P("fsdp", None),
        P("rep", "fsdp", None),
        P("rep", "fsdp", None),
    )
    out_specs = (P("fsdp", None), P("fsdp", None))
    return jax.shard_map(
        per_device, mesh=mesh, in_specs=in_specs, out_specs=out_specs, check_vma=False
    )
```

```python
import functools
import math

import jax
import jax.numpy as jnp
from jax import lax
from jax.experimental import pallas as pl
from jax.experimental.pallas import tpu as pltpu
from jax.sharding import PartitionSpec as P

D = 4096
HEAD_SIZE = 128


first_decay = 0.9
second_decay = 0.95
weight_decay = 0.1
inner_rate = 0.05
outer_rate = 0.7
momentum_keep = 0.9
epsilon = 1e-08

BF = jnp.bfloat16
F32 = jnp.float32
VMEM = pl.BlockSpec(memory_space=pltpu.VMEM)
ANY = pl.BlockSpec(memory_space=pl.ANY)
PARAMS = pltpu.CompilerParams(vmem_limit_bytes=12 * 1024 * 1024)


def cost(flops, nbytes):
    return pl.CostEstimate(flops=flops, bytes_accessed=nbytes, transcendentals=0)


def dot(a, b, dims=((1,), (0,))):
    return lax.dot_general(a, b, (dims, ((), ())), preferred_element_type=F32)


def attention_kernel(groups, per_group, queries, keys, targets, g_hi, g_lo, cross):
    seq = queries.shape[0]
    wide = per_group * seq
    source = lax.broadcasted_iota(jnp.int32, (seq, wide), 0)
    reader = lax.rem(lax.broadcasted_iota(jnp.int32, (seq, wide), 1), seq)
    causal = source <= reader
    for g in range(groups):
        cols = slice(g * HEAD_SIZE, (g + 1) * HEAD_SIZE)
        heads = [
            slice((g * per_group + h) * HEAD_SIZE, (g * per_group + h + 1) * HEAD_SIZE)
            for h in range(per_group)
        ]
        query = jnp.concatenate([queries[:, h] for h in heads], axis=0)
        target = jnp.concatenate([targets[:, h] for h in heads], axis=0)
        scores = dot(keys[:, cols], query, ((1,), (1,))) * (1.0 / math.sqrt(HEAD_SIZE))
        scores = jnp.where(causal, scores, -jnp.inf)
        expo = jnp.exp(scores - jnp.max(scores, axis=0, keepdims=True))
        probs = (expo / jnp.sum(expo, axis=0, keepdims=True)).astype(BF)
        gram = dot(probs, probs, ((1,), (1,)))
        high = gram.astype(BF)
        g_hi[:, cols] = high
        g_lo[:, cols] = (gram - high.astype(F32)).astype(BF)
        cross[:, cols] = dot(probs, target)


def own_kernel(tokens, weights, compact, own):
    compact[...] = weights[...].astype(BF)
    own[...] = dot(tokens[...], compact[...])


def partial_kernel(n, *refs):
    blocks, compact, outs = refs[:n], refs[n], refs[n + 1 :]
    for block, out in zip(blocks, outs):
        out[...] = dot(block[...], compact[...]).astype(out.dtype)


def add_kernel(one, two, out):
    out[...] = (one[...] + two[...].astype(F32)).astype(out.dtype)


def transpose_kernel(n, *refs):
    blocks, out = refs[:n], refs[n]
    seq = blocks[0].shape[0]
    for k, block in enumerate(blocks):
        out[:, k * seq : (k + 1) * seq] = block[...].T


def local(kernel, shapes, *args, flops=0, name):
    specs = [VMEM] * len(args)
    nbytes = sum(a.size * a.dtype.itemsize for a in (*args, *shapes))
    return pl.pallas_call(
        kernel,
        out_shape=tuple(shapes),
        in_specs=specs,
        out_specs=(VMEM,) * len(shapes),
        compiler_params=PARAMS,
        cost_estimate=cost(flops, nbytes),
        name=name,
    )(*args)


def after(values, *first):
    return lax.optimization_barrier((values, first))[0]


def to_chips(sends):
    return [exchange(s, "rep", 2 * k) for k, s in zip((1, 2, 3), sends)]


def value_grad_kernel(n, scale, *refs):
    own, parts = refs[0], refs[1:n]
    g_hi, g_lo, cross, out = refs[n:]
    total = own[...]
    for part in parts:
        total = total + part[...].astype(F32)
    value = (total * (1.0 / math.sqrt(D))).astype(BF)
    for g in range(out.shape[1] // HEAD_SIZE):
        cols = slice(g * HEAD_SIZE, (g + 1) * HEAD_SIZE)
        acc = dot(g_hi[:, cols], value[:, cols]) + dot(g_lo[:, cols], value[:, cols])
        out[:, cols] = ((acc - cross[:, cols]) * scale).astype(BF)


def direction_of(features, stacked, first, second, weights, at):
    summed = dot(features[at, :], stacked)
    first_new = first_decay * first[0, at, :] + (1.0 - first_decay) / math.sqrt(D) * summed
    second_new = second_decay * second[0, at, :] + (1.0 - second_decay) / D * summed * summed
    return first_new / (jnp.sqrt(second_new) + epsilon) + weight_decay * weights[at, :]


def rows_at(start, count):
    return pl.ds(pl.multiple_of(start, count), count)


def position():
    here = lax.axis_index("rep")
    return lax.div(here, 2), lax.rem(here, 2)


def first_row(other, half):
    _, core = position()
    return (1 - core if other else core) * half


def half_kernel(n, rows, other, features, *refs):
    grads = refs[:n]
    first, second, weights, out = refs[n:]
    stacked = jnp.concatenate([g[...] for g in grads], axis=0)
    start = first_row(other, weights.shape[0] // 2)
    for i in range(0, out.shape[0], rows):
        at = rows_at(start + i, rows)
        total = direction_of(features, stacked, first, second, weights, at)
        out[i : i + rows, :] = total.astype(out.dtype)


def split_kernel(mine, theirs, own, *outs):
    rows = own.shape[0]
    chip, _ = position()
    for k in range(len(outs) + 1):
        at = rows_at((chip ^ k) * rows, rows)
        total = mine[at, :] + theirs[at, :].astype(F32)
        if k == 0:
            own[...] = total
        else:
            outs[k - 1][...] = total.astype(BF)


def direction_kernel(n, features, *refs):
    grads = refs[:n]
    first, second, weights, out = refs[n:]
    stacked = jnp.concatenate([g[...] for g in grads], axis=0)
    out[...] = direction_of(features, stacked, first, second, weights, slice(None))


def mean_kernel(inv, own, *refs):
    parts, out = refs[:-1], refs[-1]
    total = own[...]
    for part in parts:
        total = total + part[...].astype(F32)
    out[...] = (total * inv).astype(BF)


def outer_kernel(mean, momentum, weights, new_weights, new_momentum):
    mean_direction = mean[...].astype(F32)
    kept = momentum_keep * momentum[...] + mean_direction
    new_momentum[...] = kept
    new_weights[...] = weights[...] - outer_rate * inner_rate * (
        mean_direction + momentum_keep * kept
    )


def piece_kernel(places, *refs):
    n = len(places)
    means, (momentum, weights) = refs[:n], refs[n : n + 2]
    new_weights, new_momentum, w_out, m_out, sems = refs[-5:]
    rows = w_out.shape[1]
    chip, _ = position()
    copies = []
    for j, (k, other) in enumerate(places):
        at = rows_at(first_row(other, weights.shape[0] // 2) + (chip ^ k) * rows, rows)
        outer_kernel(means[j], momentum.at[at, :], weights.at[at, :], w_out.at[j], m_out.at[j])
        for i, (src, dst) in enumerate(((w_out, new_weights), (m_out, new_momentum))):
            copy = pltpu.make_async_copy(src.at[j], dst.at[at, :], sems.at[i, j])
            copy.start()
            copies.append(copy)
    for copy in copies:
        copy.wait()


def outer_pieces(places, means, momentum, weights, outs):
    n = len(places)
    piece, width = means[0].shape
    full_shape = jax.ShapeDtypeStruct(weights.shape, F32)
    return pl.pallas_call(
        functools.partial(piece_kernel, places),
        out_shape=(full_shape, full_shape),
        in_specs=[VMEM] * (n + 2) + [ANY] * len(outs),
        out_specs=(ANY, ANY),
        scratch_shapes=[pltpu.VMEM((n, piece, width), F32)] * 2
        + [pltpu.SemaphoreType.DMA((2, n))],
        input_output_aliases={n + 2 + i: i for i in range(len(outs))},
        compiler_params=PARAMS,
        cost_estimate=cost(0, 18 * n * piece * width),
        name="outer_step",
    )(*means, momentum, weights, *outs)


def exchange(x, axis, k):
    n = lax.axis_size(axis)
    return lax.ppermute(x, axis, [(i, i ^ k) for i in range(n)])


def ring_hop(i, k, n):
    if n & (n - 1):
        return (i + k) % n
    place, shift = i, 1
    while shift < n:
        place = place ^ (place >> shift)
        shift *= 2
    place = (place + k) % n
    return place ^ (place >> 1)


def turn(x, k):
    n = lax.axis_size("fsdp")
    return lax.ppermute(x, "fsdp", [(i, ring_hop(i, k, n)) for i in range(n)])


def per_device(
    tokens, queries, rotated_key_rows, targets, value_weights, momentum, first_moment, second_moment
):
    seq_len = tokens.shape[0]
    rows, width = value_weights.shape
    n_seq = lax.axis_size("fsdp")
    n_rep = lax.axis_size("rep")
    groups = rotated_key_rows.shape[1] // HEAD_SIZE
    heads_per_group = queries.shape[1] // rotated_key_rows.shape[1]
    cot_scale = math.sqrt(D / (seq_len * n_seq))
    me, tokens = lax.optimization_barrier((lax.axis_index("fsdp"), tokens))
    hops = (n_seq // 2, *[k for k in range(1, n_seq) if k != n_seq // 2])

    def columns(k):
        block = ring_hop(me, k, n_seq)
        return lax.dynamic_slice(tokens, (0, block * rows), (seq_len, rows))

    cut = {hops[0]: columns(hops[0])}
    tokens, cut[hops[0]] = lax.optimization_barrier((tokens, cut[hops[0]]))
    cut.update({k: columns(k) for k in (0, *hops[1:])})
    own_block = cut[0]
    blocks = [turn(cut[k], k) for k in hops]

    block_shape = jax.ShapeDtypeStruct((seq_len, width), BF)
    wide_shape = jax.ShapeDtypeStruct((seq_len, width), F32)
    g_hi, g_lo, cross = pl.pallas_call(
        functools.partial(attention_kernel, groups, heads_per_group),
        out_shape=(block_shape, block_shape, wide_shape),
        in_specs=[VMEM] * 3,
        out_specs=(VMEM,) * 3,
        compiler_params=PARAMS,
        cost_estimate=cost(6 * seq_len * seq_len * queries.shape[1], 4 * queries.size),
        name="attention",
    )(queries, rotated_key_rows, targets)
    compact, own_value = pl.pallas_call(
        own_kernel,
        out_shape=(jax.ShapeDtypeStruct((rows, width), BF), wide_shape),
        in_specs=[VMEM] * 2,
        out_specs=(VMEM,) * 2,
        compiler_params=PARAMS,
        cost_estimate=cost(2 * seq_len * rows * width, 6 * rows * width),
        name="own_value",
    )(own_block, value_weights)

    def product(k, dtype):
        return local(
            functools.partial(partial_kernel, 1), (jax.ShapeDtypeStruct((seq_len, width), dtype),),
            blocks[hops.index(k)], compact,
            flops=2 * seq_len * rows * width, name="partial_value",
        )[0]

    if n_seq == 4:
        passed = turn(product(2, BF), 3)
        back = turn(product(3, BF), 1)
        joined = local(add_kernel, (block_shape,), product(1, F32), passed, name="joined_value")[0]
        parts = [turn(joined, 3), back]
    else:
        parts = [turn(product(k, BF), n_seq - k) for k in hops]
    features = pl.pallas_call(
        functools.partial(transpose_kernel, n_seq),
        out_shape=jax.ShapeDtypeStruct((rows, n_seq * seq_len), BF),
        in_specs=[VMEM] * n_seq,
        out_specs=VMEM,
        compiler_params=PARAMS,
        cost_estimate=cost(0, 4 * rows * n_seq * seq_len),
        name="transpose_tokens",
    )(own_block, *blocks)
    value_grad = pl.pallas_call(
        functools.partial(value_grad_kernel, 1 + len(parts), cot_scale),
        out_shape=block_shape,
        in_specs=[VMEM] * (len(parts) + 4),
        out_specs=VMEM,
        compiler_params=PARAMS,
        cost_estimate=cost(4 * seq_len * seq_len * width, 20 * seq_len * width),
        name="value_grad",
    )(own_value, *parts, g_hi, g_lo, cross)
    grads = [value_grad] + [turn(value_grad, k) for k in hops]

    moments = (first_moment, second_moment, value_weights)
    n = n_seq
    if n_rep != 8 or rows % 128:
        direction = pl.pallas_call(
            functools.partial(direction_kernel, n),
            out_shape=jax.ShapeDtypeStruct((rows, width), F32),
            in_specs=[VMEM] * (n + 4),
            out_specs=VMEM,
            compiler_params=PARAMS,
            name="direction",
        )(features, *grads, *moments)
        full_shape = jax.ShapeDtypeStruct((rows, width), F32)
        return pl.pallas_call(
            outer_kernel,
            out_shape=(full_shape, full_shape),
            in_specs=[VMEM] * 3,
            out_specs=(VMEM, VMEM),
            compiler_params=PARAMS,
            name="outer_step",
        )(lax.psum(direction, "rep") / n_rep, momentum, value_weights)

    half = rows // 2
    piece = half // 4
    small = jax.ShapeDtypeStruct((piece, width), BF)

    def half_direction(other, dtype):
        return local(
            functools.partial(half_kernel, n, min(half, 128), other),
            (jax.ShapeDtypeStruct((half, width), dtype),),
            features, *grads, *moments,
            flops=2 * half * width * features.shape[1],
            name="direction",
        )[0]

    theirs = half_direction(True, BF)
    arrived = exchange(theirs, "rep", 1)
    mine = half_direction(False, F32)
    own, *sends = local(
        split_kernel, (jax.ShapeDtypeStruct((piece, width), F32),) + (small,) * 3,
        mine, arrived, name="chip_sum",
    )
    got = to_chips(sends)
    mean = local(
        functools.partial(mean_kernel, 1.0 / n_rep), (small,), own, *got, name="mean_direction"
    )[0]
    got = to_chips([mean] * 3)
    theirs = [exchange(g, "rep", 1) for g in (mean, *got)]
    outs = outer_pieces(
        tuple((k, False) for k in range(4)), [mean, *got], momentum, value_weights, ()
    )
    return tuple(
        outer_pieces(tuple((k, True) for k in range(4)), theirs, momentum, value_weights, outs)
    )


def solution(mesh):
    in_specs = (
        P(("rep", "fsdp"), None),
        P(("rep", "fsdp"), None),
        P(("rep", "fsdp"), None),
        P(("rep", "fsdp"), None),
        P("fsdp", None),
        P("fsdp", None),
        P("rep", "fsdp", None),
        P("rep", "fsdp", None),
    )
    out_specs = (P("fsdp", None), P("fsdp", None))
    return jax.shard_map(
        per_device, mesh=mesh, in_specs=in_specs, out_specs=out_specs, check_vma=False
    )
```

```python
import functools
import math

import jax
import jax.numpy as jnp
from jax import lax
from jax.experimental import pallas as pl
from jax.experimental.pallas import tpu as pltpu
from jax.sharding import PartitionSpec as P

D = 4096
HEAD_SIZE = 128


first_decay = 0.9
second_decay = 0.95
weight_decay = 0.1
inner_rate = 0.05
outer_rate = 0.7
momentum_keep = 0.9
epsilon = 1e-08

BF = jnp.bfloat16
F32 = jnp.float32
VMEM = pl.BlockSpec(memory_space=pltpu.VMEM)
ANY = pl.BlockSpec(memory_space=pl.ANY)
PARAMS = pltpu.CompilerParams(vmem_limit_bytes=12 * 1024 * 1024)


def cost(flops, nbytes):
    return pl.CostEstimate(flops=flops, bytes_accessed=nbytes, transcendentals=0)


def dot(a, b, dims=((1,), (0,))):
    return lax.dot_general(a, b, (dims, ((), ())), preferred_element_type=F32)


def attention_kernel(groups, per_group, queries, keys, targets, g_hi, g_lo, cross):
    seq = queries.shape[0]
    wide = per_group * seq
    source = lax.broadcasted_iota(jnp.int32, (seq, wide), 0)
    reader = lax.rem(lax.broadcasted_iota(jnp.int32, (seq, wide), 1), seq)
    causal = source <= reader
    for g in range(groups):
        cols = slice(g * HEAD_SIZE, (g + 1) * HEAD_SIZE)
        heads = [
            slice((g * per_group + h) * HEAD_SIZE, (g * per_group + h + 1) * HEAD_SIZE)
            for h in range(per_group)
        ]
        query = jnp.concatenate([queries[:, h] for h in heads], axis=0)
        target = jnp.concatenate([targets[:, h] for h in heads], axis=0)
        scores = dot(keys[:, cols], query, ((1,), (1,))) * (1.0 / math.sqrt(HEAD_SIZE))
        scores = jnp.where(causal, scores, -jnp.inf)
        expo = jnp.exp(scores - jnp.max(scores, axis=0, keepdims=True))
        probs = (expo / jnp.sum(expo, axis=0, keepdims=True)).astype(BF)
        gram = dot(probs, probs, ((1,), (1,)))
        high = gram.astype(BF)
        g_hi[:, cols] = high
        g_lo[:, cols] = (gram - high.astype(F32)).astype(BF)
        cross[:, cols] = dot(probs, target)


def own_kernel(tokens, weights, compact, own):
    compact[...] = weights[...].astype(BF)
    own[...] = dot(tokens[...], compact[...])


def partial_kernel(n, *refs):
    blocks, compact, outs = refs[:n], refs[n], refs[n + 1 :]
    for block, out in zip(blocks, outs):
        out[...] = dot(block[...], compact[...]).astype(out.dtype)


def add_kernel(one, two, out):
    out[...] = (one[...] + two[...].astype(F32)).astype(out.dtype)


def transpose_kernel(n, *refs):
    blocks, out = refs[:n], refs[n]
    seq = blocks[0].shape[0]
    for k, block in enumerate(blocks):
        out[:, k * seq : (k + 1) * seq] = block[...].T


def local(kernel, shapes, *args, flops=0, name):
    specs = [VMEM] * len(args)
    nbytes = sum(a.size * a.dtype.itemsize for a in (*args, *shapes))
    return pl.pallas_call(
        kernel,
        out_shape=tuple(shapes),
        in_specs=specs,
        out_specs=(VMEM,) * len(shapes),
        compiler_params=PARAMS,
        cost_estimate=cost(flops, nbytes),
        name=name,
    )(*args)


def after(values, *first):
    return lax.optimization_barrier((values, first))[0]


def to_chips(sends):
    return [exchange(s, "rep", 2 * k) for k, s in zip((1, 2, 3), sends)]


def value_grad_kernel(n, scale, *refs):
    own, parts = refs[0], refs[1:n]
    g_hi, g_lo, cross, out = refs[n:]
    total = own[...]
    for part in parts:
        total = total + part[...].astype(F32)
    value = (total * (1.0 / math.sqrt(D))).astype(BF)
    for g in range(out.shape[1] // HEAD_SIZE):
        cols = slice(g * HEAD_SIZE, (g + 1) * HEAD_SIZE)
        acc = dot(g_hi[:, cols], value[:, cols]) + dot(g_lo[:, cols], value[:, cols])
        out[:, cols] = ((acc - cross[:, cols]) * scale).astype(BF)


def direction_of(features, stacked, first, second, weights, at):
    summed = dot(features[at, :], stacked)
    first_new = first_decay * first[0, at, :] + (1.0 - first_decay) / math.sqrt(D) * summed
    second_new = second_decay * second[0, at, :] + (1.0 - second_decay) / D * summed * summed
    root = second_new * lax.rsqrt(second_new)
    return first_new / (root + epsilon) + weight_decay * weights[at, :]


def rows_at(start, count):
    return pl.ds(pl.multiple_of(start, count), count)


def position():
    here = lax.axis_index("rep")
    return lax.div(here, 2), lax.rem(here, 2)


def first_row(other, half):
    _, core = position()
    return (1 - core if other else core) * half


def half_kernel(n, rows, other, features, *refs):
    grads = refs[:n]
    first, second, weights, out = refs[n:]
    stacked = jnp.concatenate([g[...] for g in grads], axis=0)
    start = first_row(other, weights.shape[0] // 2)
    for i in range(0, out.shape[0], rows):
        at = rows_at(start + i, rows)
        total = direction_of(features, stacked, first, second, weights, at)
        out[i : i + rows, :] = total.astype(out.dtype)


def split_kernel(mine, theirs, own, *outs):
    rows = own.shape[0]
    chip, _ = position()
    for k in range(len(outs) + 1):
        at = rows_at((chip ^ k) * rows, rows)
        total = mine[at, :] + theirs[at, :].astype(F32)
        if k == 0:
            own[...] = total
        else:
            outs[k - 1][...] = total.astype(BF)


def direction_kernel(n, features, *refs):
    grads = refs[:n]
    first, second, weights, out = refs[n:]
    stacked = jnp.concatenate([g[...] for g in grads], axis=0)
    out[...] = direction_of(features, stacked, first, second, weights, slice(None))


def mean_kernel(inv, own, *refs):
    parts, out = refs[:-1], refs[-1]
    total = own[...]
    for part in parts:
        total = total + part[...].astype(F32)
    out[...] = (total * inv).astype(BF)


def outer_kernel(mean, momentum, weights, new_weights, new_momentum):
    mean_direction = mean[...].astype(F32)
    kept = momentum_keep * momentum[...] + mean_direction
    new_momentum[...] = kept
    new_weights[...] = weights[...] - outer_rate * inner_rate * (
        mean_direction + momentum_keep * kept
    )


def piece_kernel(places, *refs):
    n = len(places)
    means, (momentum, weights) = refs[:n], refs[n : n + 2]
    new_weights, new_momentum, w_out, m_out, sems = refs[-5:]
    rows = w_out.shape[1]
    chip, _ = position()
    copies = []
    for j, (k, other) in enumerate(places):
        at = rows_at(first_row(other, weights.shape[0] // 2) + (chip ^ k) * rows, rows)
        outer_kernel(means[j], momentum.at[at, :], weights.at[at, :], w_out.at[j], m_out.at[j])
        for i, (src, dst) in enumerate(((w_out, new_weights), (m_out, new_momentum))):
            copy = pltpu.make_async_copy(src.at[j], dst.at[at, :], sems.at[i, j])
            copy.start()
            copies.append(copy)
    for copy in copies:
        copy.wait()


def outer_pieces(places, means, momentum, weights, outs):
    n = len(places)
    piece, width = means[0].shape
    full_shape = jax.ShapeDtypeStruct(weights.shape, F32)
    return pl.pallas_call(
        functools.partial(piece_kernel, places),
        out_shape=(full_shape, full_shape),
        in_specs=[VMEM] * (n + 2) + [ANY] * len(outs),
        out_specs=(ANY, ANY),
        scratch_shapes=[pltpu.VMEM((n, piece, width), F32)] * 2
        + [pltpu.SemaphoreType.DMA((2, n))],
        input_output_aliases={n + 2 + i: i for i in range(len(outs))},
        compiler_params=PARAMS,
        cost_estimate=cost(0, 18 * n * piece * width),
        name="outer_step",
    )(*means, momentum, weights, *outs)


def exchange(x, axis, k):
    n = lax.axis_size(axis)
    return lax.ppermute(x, axis, [(i, i ^ k) for i in range(n)])


def ring_hop(i, k, n):
    if n & (n - 1):
        return (i + k) % n
    place, shift = i, 1
    while shift < n:
        place = place ^ (place >> shift)
        shift *= 2
    place = (place + k) % n
    return place ^ (place >> 1)


def turn(x, k):
    n = lax.axis_size("fsdp")
    return lax.ppermute(x, "fsdp", [(i, ring_hop(i, k, n)) for i in range(n)])


def per_device(
    tokens, queries, rotated_key_rows, targets, value_weights, momentum, first_moment, second_moment
):
    seq_len = tokens.shape[0]
    rows, width = value_weights.shape
    n_seq = lax.axis_size("fsdp")
    n_rep = lax.axis_size("rep")
    groups = rotated_key_rows.shape[1] // HEAD_SIZE
    heads_per_group = queries.shape[1] // rotated_key_rows.shape[1]
    cot_scale = math.sqrt(D / (seq_len * n_seq))
    me, tokens = lax.optimization_barrier((lax.axis_index("fsdp"), tokens))
    hops = (n_seq // 2, *[k for k in range(1, n_seq) if k != n_seq // 2])

    def columns(k):
        block = ring_hop(me, k, n_seq)
        return lax.dynamic_slice(tokens, (0, block * rows), (seq_len, rows))

    cut = {hops[0]: columns(hops[0])}
    tokens, cut[hops[0]] = lax.optimization_barrier((tokens, cut[hops[0]]))
    cut.update({k: columns(k) for k in (0, *hops[1:])})
    own_block = cut[0]
    blocks = [turn(cut[k], k) for k in hops]

    block_shape = jax.ShapeDtypeStruct((seq_len, width), BF)
    wide_shape = jax.ShapeDtypeStruct((seq_len, width), F32)
    g_hi, g_lo, cross = pl.pallas_call(
        functools.partial(attention_kernel, groups, heads_per_group),
        out_shape=(block_shape, block_shape, wide_shape),
        in_specs=[VMEM] * 3,
        out_specs=(VMEM,) * 3,
        compiler_params=PARAMS,
        cost_estimate=cost(6 * seq_len * seq_len * queries.shape[1], 4 * queries.size),
        name="attention",
    )(queries, rotated_key_rows, targets)
    compact, own_value = pl.pallas_call(
        own_kernel,
        out_shape=(jax.ShapeDtypeStruct((rows, width), BF), wide_shape),
        in_specs=[VMEM] * 2,
        out_specs=(VMEM,) * 2,
        compiler_params=PARAMS,
        cost_estimate=cost(2 * seq_len * rows * width, 6 * rows * width),
        name="own_value",
    )(own_block, value_weights)

    def product(k, dtype):
        return local(
            functools.partial(partial_kernel, 1), (jax.ShapeDtypeStruct((seq_len, width), dtype),),
            blocks[hops.index(k)], compact,
            flops=2 * seq_len * rows * width, name="partial_value",
        )[0]

    if n_seq == 4:
        passed = turn(product(2, BF), 3)
        back = turn(product(3, BF), 1)
        joined = local(add_kernel, (block_shape,), product(1, F32), passed, name="joined_value")[0]
        parts = [turn(joined, 3), back]
    else:
        parts = [turn(product(k, BF), n_seq - k) for k in hops]
    features = pl.pallas_call(
        functools.partial(transpose_kernel, n_seq),
        out_shape=jax.ShapeDtypeStruct((rows, n_seq * seq_len), BF),
        in_specs=[VMEM] * n_seq,
        out_specs=VMEM,
        compiler_params=PARAMS,
        cost_estimate=cost(0, 4 * rows * n_seq * seq_len),
        name="transpose_tokens",
    )(own_block, *blocks)
    value_grad = pl.pallas_call(
        functools.partial(value_grad_kernel, 1 + len(parts), cot_scale),
        out_shape=block_shape,
        in_specs=[VMEM] * (len(parts) + 4),
        out_specs=VMEM,
        compiler_params=PARAMS,
        cost_estimate=cost(4 * seq_len * seq_len * width, 20 * seq_len * width),
        name="value_grad",
    )(own_value, *parts, g_hi, g_lo, cross)
    grads = [value_grad] + [turn(value_grad, k) for k in hops]

    moments = (first_moment, second_moment, value_weights)
    n = n_seq
    if n_rep != 8 or rows % 128:
        direction = pl.pallas_call(
            functools.partial(direction_kernel, n),
            out_shape=jax.ShapeDtypeStruct((rows, width), F32),
            in_specs=[VMEM] * (n + 4),
            out_specs=VMEM,
            compiler_params=PARAMS,
            name="direction",
        )(features, *grads, *moments)
        full_shape = jax.ShapeDtypeStruct((rows, width), F32)
        return pl.pallas_call(
            outer_kernel,
            out_shape=(full_shape, full_shape),
            in_specs=[VMEM] * 3,
            out_specs=(VMEM, VMEM),
            compiler_params=PARAMS,
            name="outer_step",
        )(lax.psum(direction, "rep") / n_rep, momentum, value_weights)

    half = rows // 2
    piece = half // 4
    small = jax.ShapeDtypeStruct((piece, width), BF)

    def half_direction(other, dtype):
        return local(
            functools.partial(half_kernel, n, min(half, 128), other),
            (jax.ShapeDtypeStruct((half, width), dtype),),
            features, *grads, *moments,
            flops=2 * half * width * features.shape[1],
            name="direction",
        )[0]

    theirs = half_direction(True, BF)
    arrived = exchange(theirs, "rep", 1)
    mine = half_direction(False, F32)
    own, *sends = local(
        split_kernel, (jax.ShapeDtypeStruct((piece, width), F32),) + (small,) * 3,
        mine, arrived, name="chip_sum",
    )
    got = to_chips(sends)
    mean = local(
        functools.partial(mean_kernel, 1.0 / n_rep), (small,), own, *got, name="mean_direction"
    )[0]
    got = to_chips([mean] * 3)
    theirs = [exchange(g, "rep", 1) for g in (mean, *got)]
    outs = outer_pieces(
        (*[(k, False) for k in range(4)], (0, True), (3, True)), [mean, *got, theirs[0], theirs[3]],
        momentum, value_weights, (),
    )
    return tuple(
        outer_pieces(((1, True), (2, True)), theirs[1:3], momentum, value_weights, outs)
    )


def solution(mesh):
    in_specs = (
        P(("rep", "fsdp"), None),
        P(("rep", "fsdp"), None),
        P(("rep", "fsdp"), None),
        P(("rep", "fsdp"), None),
        P("fsdp", None),
        P("fsdp", None),
        P("rep", "fsdp", None),
        P("rep", "fsdp", None),
    )
    out_specs = (P("fsdp", None), P("fsdp", None))
    return jax.shard_map(
        per_device, mesh=mesh, in_specs=in_specs, out_specs=out_specs, check_vma=False
    )
```

```python
import functools
import math

import jax
import jax.numpy as jnp
from jax import lax
from jax.experimental import pallas as pl
from jax.experimental.pallas import tpu as pltpu
from jax.sharding import PartitionSpec as P

D = 4096
HEAD_SIZE = 128


first_decay = 0.9
second_decay = 0.95
weight_decay = 0.1
inner_rate = 0.05
outer_rate = 0.7
momentum_keep = 0.9
epsilon = 1e-08

BF = jnp.bfloat16
F32 = jnp.float32
VMEM = pl.BlockSpec(memory_space=pltpu.VMEM)
ANY = pl.BlockSpec(memory_space=pl.ANY)
PARAMS = pltpu.CompilerParams(vmem_limit_bytes=12 * 1024 * 1024)


def cost(flops, nbytes):
    return pl.CostEstimate(flops=flops, bytes_accessed=nbytes, transcendentals=0)


def dot(a, b, dims=((1,), (0,))):
    return lax.dot_general(a, b, (dims, ((), ())), preferred_element_type=F32)


def attention_kernel(groups, per_group, queries, keys, targets, g_hi, g_lo, cross):
    seq = queries.shape[0]
    wide = per_group * seq
    source = lax.broadcasted_iota(jnp.int32, (seq, wide), 0)
    reader = lax.rem(lax.broadcasted_iota(jnp.int32, (seq, wide), 1), seq)
    causal = source <= reader
    for g in range(groups):
        cols = slice(g * HEAD_SIZE, (g + 1) * HEAD_SIZE)
        heads = [
            slice((g * per_group + h) * HEAD_SIZE, (g * per_group + h + 1) * HEAD_SIZE)
            for h in range(per_group)
        ]
        query = jnp.concatenate([queries[:, h] for h in heads], axis=0)
        target = jnp.concatenate([targets[:, h] for h in heads], axis=0)
        scores = dot(keys[:, cols], query, ((1,), (1,))) * (1.0 / math.sqrt(HEAD_SIZE))
        scores = jnp.where(causal, scores, -jnp.inf)
        expo = jnp.exp(scores - jnp.max(scores, axis=0, keepdims=True))
        probs = (expo / jnp.sum(expo, axis=0, keepdims=True)).astype(BF)
        gram = dot(probs, probs, ((1,), (1,)))
        high = gram.astype(BF)
        g_hi[:, cols] = high
        g_lo[:, cols] = (gram - high.astype(F32)).astype(BF)
        cross[:, cols] = dot(probs, target)


def own_kernel(tokens, weights, compact, own):
    compact[...] = weights[...].astype(BF)
    own[...] = dot(tokens[...], compact[...])


def partial_kernel(n, *refs):
    blocks, compact, outs = refs[:n], refs[n], refs[n + 1 :]
    for block, out in zip(blocks, outs):
        out[...] = dot(block[...], compact[...]).astype(out.dtype)


def add_kernel(one, two, out):
    out[...] = (one[...] + two[...].astype(F32)).astype(out.dtype)


def transpose_kernel(n, *refs):
    blocks, out = refs[:n], refs[n]
    seq = blocks[0].shape[0]
    for k, block in enumerate(blocks):
        out[:, k * seq : (k + 1) * seq] = block[...].T


def local(kernel, shapes, *args, flops=0, name):
    specs = [VMEM] * len(args)
    nbytes = sum(a.size * a.dtype.itemsize for a in (*args, *shapes))
    return pl.pallas_call(
        kernel,
        out_shape=tuple(shapes),
        in_specs=specs,
        out_specs=(VMEM,) * len(shapes),
        compiler_params=PARAMS,
        cost_estimate=cost(flops, nbytes),
        name=name,
    )(*args)


def after(values, *first):
    return lax.optimization_barrier((values, first))[0]


def to_chips(sends):
    return [exchange(s, "rep", 2 * k) for k, s in zip((1, 2, 3), sends)]


def value_grad_kernel(n, scale, *refs):
    own, parts = refs[0], refs[1:n]
    g_hi, g_lo, cross, out = refs[n:]
    total = own[...]
    for part in parts:
        total = total + part[...].astype(F32)
    value = (total * (1.0 / math.sqrt(D))).astype(BF)
    for g in range(out.shape[1] // HEAD_SIZE):
        cols = slice(g * HEAD_SIZE, (g + 1) * HEAD_SIZE)
        both = jnp.concatenate([g_hi[:, cols], g_lo[:, cols]], axis=1)
        acc = dot(both, jnp.concatenate([value[:, cols]] * 2, axis=0))
        out[:, cols] = ((acc - cross[:, cols]) * scale).astype(BF)


def direction_of(features, stacked, first, second, weights, at):
    summed = dot(features[at, :], stacked)
    first_new = first_decay * first[0, at, :] + (1.0 - first_decay) / math.sqrt(D) * summed
    second_new = second_decay * second[0, at, :] + (1.0 - second_decay) / D * summed * summed
    root = second_new * lax.rsqrt(second_new)
    return first_new / (root + epsilon) + weight_decay * weights[at, :]


def rows_at(start, count):
    return pl.ds(pl.multiple_of(start, count), count)


def position():
    here = lax.axis_index("rep")
    return lax.div(here, 2), lax.rem(here, 2)


def first_row(other, half):
    _, core = position()
    return (1 - core if other else core) * half


def half_kernel(n, rows, other, features, *refs):
    grads = refs[:n]
    first, second, weights, out = refs[n:]
    stacked = jnp.concatenate([g[...] for g in grads], axis=0)
    start = first_row(other, weights.shape[0] // 2)
    for i in range(0, out.shape[0], rows):
        at = rows_at(start + i, rows)
        total = direction_of(features, stacked, first, second, weights, at)
        out[i : i + rows, :] = total.astype(out.dtype)


def split_kernel(mine, theirs, own, *outs):
    rows = own.shape[0]
    chip, _ = position()
    for k in range(len(outs) + 1):
        at = rows_at((chip ^ k) * rows, rows)
        total = mine[at, :] + theirs[at, :].astype(F32)
        if k == 0:
            own[...] = total
        else:
            outs[k - 1][...] = total.astype(BF)


def direction_kernel(n, features, *refs):
    grads = refs[:n]
    first, second, weights, out = refs[n:]
    stacked = jnp.concatenate([g[...] for g in grads], axis=0)
    out[...] = direction_of(features, stacked, first, second, weights, slice(None))


def mean_kernel(inv, own, *refs):
    parts, out = refs[:-1], refs[-1]
    total = own[...]
    for part in parts:
        total = total + part[...].astype(F32)
    out[...] = (total * inv).astype(BF)


def outer_kernel(mean, momentum, weights, new_weights, new_momentum):
    mean_direction = mean[...].astype(F32)
    kept = momentum_keep * momentum[...] + mean_direction
    new_momentum[...] = kept
    new_weights[...] = weights[...] - outer_rate * inner_rate * (
        mean_direction + momentum_keep * kept
    )


def piece_kernel(places, *refs):
    n = len(places)
    means, (momentum, weights) = refs[:n], refs[n : n + 2]
    new_weights, new_momentum, w_out, m_out, sems = refs[-5:]
    rows = w_out.shape[1]
    chip, _ = position()
    copies = []
    for j, (k, other) in enumerate(places):
        at = rows_at(first_row(other, weights.shape[0] // 2) + (chip ^ k) * rows, rows)
        outer_kernel(means[j], momentum.at[at, :], weights.at[at, :], w_out.at[j], m_out.at[j])
        for i, (src, dst) in enumerate(((w_out, new_weights), (m_out, new_momentum))):
            copy = pltpu.make_async_copy(src.at[j], dst.at[at, :], sems.at[i, j])
            copy.start()
            copies.append(copy)
    for copy in copies:
        copy.wait()


def outer_pieces(places, means, momentum, weights, outs):
    n = len(places)
    piece, width = means[0].shape
    full_shape = jax.ShapeDtypeStruct(weights.shape, F32)
    return pl.pallas_call(
        functools.partial(piece_kernel, places),
        out_shape=(full_shape, full_shape),
        in_specs=[VMEM] * (n + 2) + [ANY] * len(outs),
        out_specs=(ANY, ANY),
        scratch_shapes=[pltpu.VMEM((n, piece, width), F32)] * 2
        + [pltpu.SemaphoreType.DMA((2, n))],
        input_output_aliases={n + 2 + i: i for i in range(len(outs))},
        compiler_params=PARAMS,
        cost_estimate=cost(0, 18 * n * piece * width),
        name="outer_step",
    )(*means, momentum, weights, *outs)


def exchange(x, axis, k):
    n = lax.axis_size(axis)
    return lax.ppermute(x, axis, [(i, i ^ k) for i in range(n)])


def ring_hop(i, k, n):
    if n & (n - 1):
        return (i + k) % n
    place, shift = i, 1
    while shift < n:
        place = place ^ (place >> shift)
        shift *= 2
    place = (place + k) % n
    return place ^ (place >> 1)


def turn(x, k):
    n = lax.axis_size("fsdp")
    return lax.ppermute(x, "fsdp", [(i, ring_hop(i, k, n)) for i in range(n)])


def per_device(
    tokens, queries, rotated_key_rows, targets, value_weights, momentum, first_moment, second_moment
):
    seq_len = tokens.shape[0]
    rows, width = value_weights.shape
    n_seq = lax.axis_size("fsdp")
    n_rep = lax.axis_size("rep")
    groups = rotated_key_rows.shape[1] // HEAD_SIZE
    heads_per_group = queries.shape[1] // rotated_key_rows.shape[1]
    cot_scale = math.sqrt(D / (seq_len * n_seq))
    me, tokens = lax.optimization_barrier((lax.axis_index("fsdp"), tokens))
    hops = (n_seq // 2, *[k for k in range(1, n_seq) if k != n_seq // 2])

    def columns(k):
        block = ring_hop(me, k, n_seq)
        return lax.dynamic_slice(tokens, (0, block * rows), (seq_len, rows))

    cut = {hops[0]: columns(hops[0])}
    tokens, cut[hops[0]] = lax.optimization_barrier((tokens, cut[hops[0]]))
    cut.update({k: columns(k) for k in (0, *hops[1:])})
    own_block = cut[0]
    blocks = [turn(cut[k], k) for k in hops]

    block_shape = jax.ShapeDtypeStruct((seq_len, width), BF)
    wide_shape = jax.ShapeDtypeStruct((seq_len, width), F32)
    g_hi, g_lo, cross = pl.pallas_call(
        functools.partial(attention_kernel, groups, heads_per_group),
        out_shape=(block_shape, block_shape, wide_shape),
        in_specs=[VMEM] * 3,
        out_specs=(VMEM,) * 3,
        compiler_params=PARAMS,
        cost_estimate=cost(6 * seq_len * seq_len * queries.shape[1], 4 * queries.size),
        name="attention",
    )(queries, rotated_key_rows, targets)
    compact, own_value = pl.pallas_call(
        own_kernel,
        out_shape=(jax.ShapeDtypeStruct((rows, width), BF), wide_shape),
        in_specs=[VMEM] * 2,
        out_specs=(VMEM,) * 2,
        compiler_params=PARAMS,
        cost_estimate=cost(2 * seq_len * rows * width, 6 * rows * width),
        name="own_value",
    )(own_block, value_weights)

    def product(k, dtype):
        return local(
            functools.partial(partial_kernel, 1), (jax.ShapeDtypeStruct((seq_len, width), dtype),),
            blocks[hops.index(k)], compact,
            flops=2 * seq_len * rows * width, name="partial_value",
        )[0]

    if n_seq == 4:
        passed = turn(product(2, BF), 3)
        back = turn(product(3, BF), 1)
        joined = local(add_kernel, (block_shape,), product(1, F32), passed, name="joined_value")[0]
        parts = [turn(joined, 3), back]
    else:
        parts = [turn(product(k, BF), n_seq - k) for k in hops]
    features = pl.pallas_call(
        functools.partial(transpose_kernel, n_seq),
        out_shape=jax.ShapeDtypeStruct((rows, n_seq * seq_len), BF),
        in_specs=[VMEM] * n_seq,
        out_specs=VMEM,
        compiler_params=PARAMS,
        cost_estimate=cost(0, 4 * rows * n_seq * seq_len),
        name="transpose_tokens",
    )(own_block, *blocks)
    value_grad = pl.pallas_call(
        functools.partial(value_grad_kernel, 1 + len(parts), cot_scale),
        out_shape=block_shape,
        in_specs=[VMEM] * (len(parts) + 4),
        out_specs=VMEM,
        compiler_params=PARAMS,
        cost_estimate=cost(4 * seq_len * seq_len * width, 20 * seq_len * width),
        name="value_grad",
    )(own_value, *parts, g_hi, g_lo, cross)
    grads = [value_grad] + [turn(value_grad, k) for k in hops]

    moments = (first_moment, second_moment, value_weights)
    n = n_seq
    if n_rep != 8 or rows % 128:
        direction = pl.pallas_call(
            functools.partial(direction_kernel, n),
            out_shape=jax.ShapeDtypeStruct((rows, width), F32),
            in_specs=[VMEM] * (n + 4),
            out_specs=VMEM,
            compiler_params=PARAMS,
            name="direction",
        )(features, *grads, *moments)
        full_shape = jax.ShapeDtypeStruct((rows, width), F32)
        return pl.pallas_call(
            outer_kernel,
            out_shape=(full_shape, full_shape),
            in_specs=[VMEM] * 3,
            out_specs=(VMEM, VMEM),
            compiler_params=PARAMS,
            name="outer_step",
        )(lax.psum(direction, "rep") / n_rep, momentum, value_weights)

    half = rows // 2
    piece = half // 4
    small = jax.ShapeDtypeStruct((piece, width), BF)

    def half_direction(other, dtype):
        return local(
            functools.partial(half_kernel, n, min(half, 128), other),
            (jax.ShapeDtypeStruct((half, width), dtype),),
            features, *grads, *moments,
            flops=2 * half * width * features.shape[1],
            name="direction",
        )[0]

    theirs = half_direction(True, BF)
    arrived = exchange(theirs, "rep", 1)
    mine = half_direction(False, F32)
    own, *sends = local(
        split_kernel, (jax.ShapeDtypeStruct((piece, width), F32),) + (small,) * 3,
        mine, arrived, name="chip_sum",
    )
    got = to_chips(sends)
    mean = local(
        functools.partial(mean_kernel, 1.0 / n_rep), (small,), own, *got, name="mean_direction"
    )[0]
    got = to_chips([mean] * 3)
    theirs = [exchange(g, "rep", 1) for g in (mean, *got)]
    outs = outer_pieces(
        (*[(k, False) for k in range(4)], (0, True), (3, True)), [mean, *got, theirs[0], theirs[3]],
        momentum, value_weights, (),
    )
    return tuple(
        outer_pieces(((1, True), (2, True)), theirs[1:3], momentum, value_weights, outs)
    )


def solution(mesh):
    in_specs = (
        P(("rep", "fsdp"), None),
        P(("rep", "fsdp"), None),
        P(("rep", "fsdp"), None),
        P(("rep", "fsdp"), None),
        P("fsdp", None),
        P("fsdp", None),
        P("rep", "fsdp", None),
        P("rep", "fsdp", None),
    )
    out_specs = (P("fsdp", None), P("fsdp", None))
    return jax.shard_map(
        per_device, mesh=mesh, in_specs=in_specs, out_specs=out_specs, check_vma=False
    )
```
